512 devices in a mesh: state: 32 (over z, y_hi), member: 16 (over y_lo, x, core).
Axes of the slice: x: 4, y: 4 (y_hi: 2, y_lo: 2; y = y_hi * 2 + y_lo), z: 16, core: 2. Of those that a mesh axis runs over, the one named last changes fastest.
Arguments:
- base_state: float32 [131072], P('state'), may hold values from -6 to 6
- anomalies: bfloat16 [1024, 131072], P('member', 'state'), may hold values from -6 to 6
- transform: bfloat16 [1024, 1024], P('member')
- weights: float32 [1024], P('member'), may hold values from -6 to 6
- observed: float32 [131072], P('state'), may hold values from -6 to 6
- obs_scale: float32 [131072], P('state'), may hold values from 0.1 to 1
- obs_rows: int32 [131072], P('state'), may hold values from 0 to 131071, as said below
- offsets: int32 [8], replicated, may hold values from -512 to 512, as said below
Outputs:
- hessian: float32 [1024, 1024], P('member', 'state')
- gradient: float32 [1024], P('member')
The draws below stay inside these ranges and needn't reach their ends.
Inputs may be any that keep to these rules, and one draw needn't show every extreme that they name: `obs_rows`: observation o with p * 4096 <= o < (p + 1) * 4096 lies in state rows p * 4096 to (p + 1) * 4096 - 1; observation 0 is at row 0 and observation 131072 - 1 at row 131071. offsets -512 and 512 both occur.
All inputs are finite; a program needn't handle non-finite values.
Results may differ from the reference program's by a relative error of at most 0.0042.
Values may be sent and summed in bfloat16 or wider, within the bound.
No kernel may reach another device: no remote copies, remote signals or barrier semaphores. Data moves between devices by JAX's collectives and lax.ppermute only.
A program may use at most 64 MiB of HBM per device.

```python
import math
import jax
import jax.numpy as jnp
from jax import lax

M = 1024
S_DEV = 4096
OBS_DEV = 4096
K = 8
REACH = 512
NS = 131072
NOBS = 131072


def draw_transform(key, part):
    key = jax.random.fold_in(key, 13)
    random_part = jax.random.normal(key, (M, M), jnp.float32)
    return (jnp.eye(M, dtype=jnp.float32) + 0.7 / math.sqrt(M) * random_part).astype(jnp.bfloat16)


def draw_obs_rows(key, part):
    key = jax.random.fold_in(key, 11)
    within = jax.random.randint(key, (NOBS,), 0, S_DEV)
    block_index = jnp.arange(NOBS, dtype=jnp.int32) // OBS_DEV
    row_index = block_index * S_DEV + within
    row_index = row_index.at[0].set(0).at[NOBS - 1].set(NS - 1)
    return row_index.astype(jnp.int32)


def draw_offsets(key, part):
    key = jax.random.fold_in(key, 12)
    values = jax.random.randint(key, (K,), -REACH, REACH + 1)
    values = values.at[0].set(-REACH).at[1].set(REACH)
    return values.astype(jnp.int32)


def block_levels(key, shape, shards, least, largest):
    def one(position, shards_of):
        draws = jax.random.uniform(jax.random.fold_in(jax.random.fold_in(key, 6), position), (shards_of,), jnp.float32, least / len(shards), largest / len(shards))
        return jnp.repeat(jnp.exp(draws), shape[position] // shards_of).reshape((-1,) + (1,) * (len(shape) - position - 1))

    factor_of = one(*shards[0])
    for cut in shards[1:]:
        factor_of = factor_of * one(*cut)
    return factor_of


def gaussian(own_key, extent, deviation, bound, split=(), held_as=jnp.bfloat16):
    array = jax.random.normal(own_key, extent, jnp.float32) * deviation
    if len(split) > 0:
        array = block_levels(own_key, extent, split, -0.22, 0.18) * array
    return jnp.clip(array, min=-bound, max=bound).astype(held_as)


def setup_inputs(seed: int = 0) -> dict:
    splits = jax.random.split(jax.random.key(seed), 9)
    return {
        "base_state": gaussian(splits[0], (NS,), 1.0, 6.0, ((0, 32),), jnp.float32),
        "anomalies": gaussian(splits[1], (M, NS), 1.0, 6.0, ((0, 16), (1, 32))),
        "transform": draw_transform(jax.random.fold_in(splits[8], 71), 0),
        "weights": gaussian(splits[3], (M,), 1.0, 6.0, ((0, 16),), jnp.float32),
        "observed": gaussian(splits[4], (NOBS,), 1.0, 6.0, ((0, 32),), jnp.float32),
        "obs_scale": jnp.clip(jnp.exp(math.log(1.0) - 2.3025851 * jax.random.uniform(splits[5], (NOBS,), jnp.float32) ** block_levels(splits[5], (NOBS,), ((0, 32),), -0.2, 0.2)), 0.1, 1.0),
        "obs_rows": draw_obs_rows(jax.random.fold_in(splits[8], 71), 0),
        "offsets": draw_offsets(jax.random.fold_in(splits[8], 71), 0),
    }


def reference(base_state, anomalies, transform, weights, observed, obs_scale, obs_rows, offsets):
    mixed_states = jnp.dot(transform.astype(jnp.float32), anomalies.astype(jnp.float32), precision=lax.Precision.HIGHEST)
    ensemble = (mixed_states + base_state[None, :]).astype(jnp.bfloat16)
    padded = jnp.pad(ensemble, ((0, 0), (REACH, REACH)))
    stencil_mean = jnp.zeros((M, NOBS), jnp.float32)
    for tap_index in range(K):
        stencil_mean = stencil_mean + padded[:, obs_rows + REACH + offsets[tap_index]].astype(jnp.float32)
    stencil_mean = stencil_mean / K
    predicted = stencil_mean + 0.25 * stencil_mean * stencil_mean
    obs_average = lax.optimization_barrier(jnp.sum(predicted, axis=0)) / M
    scaled = (obs_scale * (predicted - obs_average) / math.sqrt(M - 1)).astype(jnp.bfloat16)
    innovation = obs_scale * (observed - obs_average)
    scaled_wide = scaled.astype(jnp.float32)
    hessian = jnp.eye(M, dtype=jnp.float32) + jnp.dot(scaled_wide, scaled_wide.T, precision=lax.Precision.HIGHEST)
    gradient = weights - jnp.dot(scaled_wide, innovation, precision=lax.Precision.HIGHEST)
    return (hessian, gradient)
```

```python
import math

import jax
import jax.numpy as jnp
from jax import lax
from jax.experimental import pallas as pl
from jax.experimental.pallas import tpu as pltpu
from jax.sharding import Mesh, PartitionSpec as P

M = 1024
S = 4096
REACH = 512
TAPS = 8
ROWS = 64
BF = jnp.bfloat16
F32 = jnp.float32
NT = (((1,), (1,)), ((), ()))
VMEM_LIMIT = 50 * 1024 * 1024


def call(kernel, out_shape, in_specs, scratch=(), flops=0, nbytes=0):
    return pl.pallas_call(
        kernel,
        out_shape=out_shape,
        in_specs=in_specs,
        out_specs=jax.tree.map(lambda _: pl.BlockSpec(memory_space=pltpu.VMEM), out_shape),
        scratch_shapes=list(scratch),
        compiler_params=pltpu.CompilerParams(vmem_limit_bytes=VMEM_LIMIT),
        cost_estimate=pl.CostEstimate(flops=flops, bytes_accessed=nbytes, transcendentals=0),
    )


def vmem():
    return pl.BlockSpec(memory_space=pltpu.VMEM)


def smem():
    return pl.BlockSpec(memory_space=pltpu.SMEM)


def three_parts(value):
    high = value.astype(BF)
    rest = value - high.astype(F32)
    middle = rest.astype(BF)
    low = (rest - middle.astype(F32)).astype(BF)
    return high, middle, low


def base_rows(base):
    high, middle, low = three_parts(base)
    zeros = jnp.zeros((13, base.shape[1]), BF)
    return jnp.concatenate([high, middle, low, zeros], axis=0)


def pack_kernel(place, anomalies, base, to_core, edge_own, edge_other):
    core = place[0]
    wide = S // 2 + REACH

    @pl.when(core == 0)
    def _():
        to_core[...] = anomalies[:, S - wide :]
        edge_own[0:ROWS] = anomalies[:, S - REACH :]
        edge_own[ROWS:] = base_rows(base[:, S - REACH :])
        edge_other[...] = anomalies[:, :REACH]

    @pl.when(core == 1)
    def _():
        to_core[...] = anomalies[:, :wide]
        edge_own[0:ROWS] = anomalies[:, :REACH]
        edge_own[ROWS:] = base_rows(base[:, :REACH])
        edge_other[...] = anomalies[:, S - REACH :]


CH = 256
PITCH = 144
NCH = 12


def stencil_kernel(
    place, offsets, anomalies, base, from_core, edge_own, edge_other, keep, send, base_mean, rows
):
    core = place[0]
    y_lo = place[1]
    wide = S // 2 + REACH

    def fill(chunk, first, second, extra):
        at = chunk * PITCH
        rows[at : at + ROWS] = first
        rows[at + ROWS : at + 2 * ROWS] = second
        rows[at + 2 * ROWS : at + PITCH] = extra

    @pl.when(core == 0)
    def _():
        for k in range(2):
            c = slice(k * CH, k * CH + CH)
            fill(k, edge_own[0:ROWS, c], edge_other[:, c], edge_own[ROWS:, c])
        for k in range(wide // CH):
            c = slice(k * CH, k * CH + CH)
            fill(k + 2, anomalies[:, c], from_core[:, c], base_rows(base[:, c]))

    @pl.when(core == 1)
    def _():
        for k in range(wide // CH):
            c = slice(k * CH, k * CH + CH)
            d = slice(S - wide + k * CH, S - wide + k * CH + CH)
            fill(k, from_core[:, c], anomalies[:, d], base_rows(base[:, d]))
        for k in range(2):
            c = slice(k * CH, k * CH + CH)
            fill(k + wide // CH, edge_other[:, c], edge_own[0:ROWS, c], edge_own[ROWS:, c])

    total = jnp.zeros((8 * PITCH, CH), F32)
    for k in range(5):
        shift = (
            lax.broadcasted_iota(jnp.int32, (CH, CH), 0)
            - lax.broadcasted_iota(jnp.int32, (CH, CH), 1)
            + (k * CH - REACH)
        )
        count = jnp.zeros((CH, CH), F32)
        for tap in range(TAPS):
            count = count + jnp.where(shift == offsets[tap], 1.0 / TAPS, 0.0)
        total = total + jnp.dot(
            rows[k * PITCH : (k + 8) * PITCH], count.astype(BF), preferred_element_type=F32
        )

    def put(target, half):
        for j in range(4):
            at = (half * 4 + j) * PITCH
            target[:, j * CH : j * CH + CH] = total[at : at + 2 * ROWS].astype(BF)

    def put_base(half):
        for j in range(4):
            at = (half * 4 + j) * PITCH + 2 * ROWS
            base_mean[:, j * CH : j * CH + CH] = (
                total[at : at + 1] + total[at + 1 : at + 2] + total[at + 2 : at + 3]
            )

    @pl.when(y_lo == 0)
    def _():
        put(keep, 0)
        put(send, 1)
        put_base(0)

    @pl.when(y_lo == 1)
    def _():
        put(keep, 1)
        put(send, 0)
        put_base(1)


def weight_kernel(place, observed, obs_scale, obs_rows, weight_row, value_row):
    first = place[2]
    scale = obs_scale[...]
    square = scale * scale
    value = square * observed[...]
    at = obs_rows[...] - first
    high = at >> 7
    low = at & 127
    inside = (at >= 0) & (at < S // 4)
    lanes = lax.broadcasted_iota(jnp.int32, (128, S), 0) == low
    lanes = jnp.where(lanes, 1.0, 0.0).astype(BF)
    blocks = (lax.broadcasted_iota(jnp.int32, (8, S), 0) == high) & inside
    parts = []
    for term in (square, value):
        for part in three_parts(term):
            parts.append(jnp.where(blocks, part.astype(F32), 0.0))
    left = jnp.concatenate(parts, axis=0).astype(BF)
    sums = lax.dot_general(left, lanes, NT, preferred_element_type=F32)
    weight = sums[0:8] + sums[8:16] + sums[16:24]
    worth = sums[24:32] + sums[32:40] + sums[40:48]
    for k in range(8):
        weight_row[:, k * 128 : k * 128 + 128] = weight[k : k + 1]
        value_row[:, k * 128 : k * 128 + 128] = worth[k : k + 1]


def two_part_rows(value, spare):
    high = value.astype(BF).astype(F32)
    low = value - high
    row = jnp.concatenate([high, low], axis=1)
    return jnp.concatenate([row, jnp.zeros((spare - 1, 128), F32)], axis=0).astype(BF)


def gram_kernel(
    place, transform, b00, b01, b10, b11, b20, b21, b30, b31, base_mean, weight_row, value_row,
    out, gathered, centred, scaled, part,
):
    y_lo = place[1]
    x = place[3]
    for step, pair in enumerate(((b00, b01), (b10, b11), (b20, b21), (b30, b31))):
        other = lax.rem(x + (0, 3, 1, 2)[step], 4)
        for side in range(2):
            y = y_lo if side == 0 else 1 - y_lo
            at = pl.multiple_of(y * 512 + other * 128, 128)
            gathered[pl.ds(at, 128)] = pair[side][...]

    mine = (pl.multiple_of(x * 128, 128), pl.multiple_of(512 + x * 128, 128))
    part[...] = jnp.zeros_like(part)
    for k in range(4):
        c = slice(k * CH, k * CH + CH)
        mean = jnp.dot(transform[...], gathered[:, c], preferred_element_type=F32)
        mean = mean + base_mean[:, c]
        predicted = mean + 0.25 * mean * mean
        average = jnp.sum(predicted, axis=0, keepdims=True) * (1.0 / M)
        difference = predicted - average
        centred[...] = difference
        weight = weight_row[:, c]
        scaled[:, c] = (difference * jnp.sqrt(weight * (1.0 / (M - 1)))).astype(BF)
        slope = (value_row[:, c] - weight * average) * (1.0 / math.sqrt(M - 1))
        for side in range(2):
            part[side * 128 : side * 128 + 128] += (
                centred[pl.ds(mine[side], 128)] * slope
            )
    rows = jnp.concatenate([scaled[pl.ds(mine[0], 128)], scaled[pl.ds(mine[1], 128)]], axis=0)
    gram = lax.dot_general(scaled[...], rows, NT, preferred_element_type=F32)
    left_half = lax.broadcasted_iota(jnp.int32, (16, 128), 1) < 64
    slopes = jnp.sum(part[...].T, axis=0, keepdims=True)
    for y in range(2):
        lanes = slice(y * 128, y * 128 + 128)
        sums = slopes[:, lanes]
        for core in range(2):
            tail = two_part_rows(sums[:, core * 64 : core * 64 + 64], 16)
            for y_hi in range(2):
                target = out.at[y_hi * 4 + y * 2 + core]
                for z in range(16):
                    at = z * 64 + y_hi * 32
                    top = gram[at : at + 16, lanes]
                    bottom = gram[at + 16 : at + 32, lanes]
                    if core == 0:
                        packed = jnp.where(left_half, top, pltpu.roll(bottom, 64, 1))
                    else:
                        packed = jnp.where(left_half, pltpu.roll(top, 64, 1), bottom)
                    target[z * 16 : z * 16 + 16] = packed.astype(BF)
                target[256:272] = tail


def middle_kernel(parts, out):
    total = jnp.sum(parts[...].astype(F32), axis=0)
    slopes = total[256:257]
    tail = jnp.concatenate([slopes, jnp.zeros((7, 128), F32)], axis=0)
    for z in range(16):
        out[z, 0:16] = total[z * 16 : z * 16 + 16]
        out[z, 16:24] = tail


def last_kernel(place, parts, weights, hessian, gradient):
    total = jnp.sum(parts[...], axis=0)
    packed = total[0:16]
    tall = jnp.concatenate([packed, jnp.zeros((112, 128), F32)], axis=0).T
    block = jnp.concatenate([tall[0:64, 0:16], tall[64:128, 0:16]], axis=1)
    row = lax.broadcasted_iota(jnp.int32, (ROWS, 32), 0) + place[4]
    column = lax.broadcasted_iota(jnp.int32, (ROWS, 32), 1) + place[5]
    hessian[...] = block + jnp.where(row == column, 1.0, 0.0)
    slopes = total[16:17, 0:64] + total[16:17, 64:128]
    gradient[...] = weights[...] - slopes


def on_device(base_state, anomalies, transform, weights, observed, obs_scale, obs_rows, offsets):
    z = lax.axis_index("z")
    y_hi = lax.axis_index("y_hi")
    y_lo = lax.axis_index("y_lo")
    x = lax.axis_index("x")
    core = lax.axis_index("core")
    state = z * 2 + y_hi
    column0 = state * S + core * (S // 2) + y_lo * (S // 4)
    place = jnp.stack(
        [core, y_lo, column0, x, (y_lo * 8 + x * 2 + core) * ROWS, state * 32]
    ).astype(jnp.int32)
    base = base_state.reshape(1, S)

    whole_transform = lax.all_gather(transform, ("y_lo", "x", "core"), axis=0, tiled=True)

    shape = lambda *s: jax.ShapeDtypeStruct(s, BF)
    wide = S // 2 + REACH
    to_core, edge_own, edge_other = call(
        pack_kernel,
        (shape(ROWS, wide), shape(ROWS + 16, REACH), shape(ROWS, REACH)),
        [smem(), vmem(), vmem()],
        nbytes=2**20,
    )(place, anomalies, base)

    swap = [(0, 1), (1, 0)]
    own_pairs = [(s * 2, s * 2 + 2) for s in range(31)] + [
        (s * 2 + 1, s * 2 - 1) for s in range(1, 32)
    ]
    other_pairs = [(s * 2 + 1, s * 2 + 2) for s in range(31)] + [
        (s * 2, s * 2 - 1) for s in range(1, 32)
    ]
    from_core = lax.ppermute(to_core, "core", swap)
    edge_own = lax.ppermute(edge_own, ("z", "y_hi", "core"), own_pairs)
    edge_other = lax.ppermute(edge_other, ("z", "y_hi", "core"), other_pairs)

    row = lambda v: v.reshape(1, S)
    f32 = lambda *s: jax.ShapeDtypeStruct(s, F32)
    weight_row, value_row = call(
        weight_kernel,
        (f32(1, S // 4), f32(1, S // 4)),
        [smem(), vmem(), vmem(), vmem()],
        flops=2 * 48 * S * 128,
        nbytes=2**20,
    )(place, row(observed), row(obs_scale), row(obs_rows))

    keep, send, base_mean = call(
        stencil_kernel,
        (shape(128, S // 4), shape(128, S // 4), f32(1, S // 4)),
        [smem(), smem()] + [vmem()] * 5,
        scratch=[pltpu.VMEM((NCH * PITCH, CH), BF)],
        flops=2 * 1152 * 1280 * 256,
        nbytes=2**21,
    )(place, offsets, anomalies, base, from_core, edge_own, edge_other)

    ring = lambda d: [(i, (i + d) % 4) for i in range(4)]
    got = lax.ppermute(send, "y_lo", swap)
    left = lax.ppermute(keep, "x", ring(1))
    right = lax.ppermute(keep, "x", ring(3))
    left_got = lax.ppermute(got, "x", ring(1))
    right_got = lax.ppermute(got, "x", ring(3))
    far = lax.ppermute(left, "x", ring(1))
    far_got = lax.ppermute(right_got, "x", ring(3))

    parts = call(
        gram_kernel,
        shape(8, 272, 128),
        [smem()] + [vmem()] * 12,
        scratch=[
            pltpu.VMEM((M, S // 4), BF),
            pltpu.VMEM((M, CH), F32),
            pltpu.VMEM((M, S // 4), BF),
            pltpu.VMEM((256, CH), F32),
        ],
        flops=2 * M * M * 1280,
        nbytes=2**22,
    )(
        place, whole_transform, keep, got, left, left_got, right, right_got, far, far_got,
        base_mean, weight_row, value_row,
    )
    parts = lax.all_to_all(parts, ("y_hi", "y_lo", "core"), 0, 0)
    sums = call(middle_kernel, f32(16, 24, 128), [vmem()], nbytes=2**19)(parts)
    sums = lax.all_to_all(sums, "z", 0, 0)
    hessian, gradient = call(
        last_kernel, (f32(ROWS, 32), f32(1, ROWS)), [smem(), vmem(), vmem()], nbytes=2**18
    )(place, sums, weights.reshape(1, ROWS))
    return hessian, gradient.reshape(ROWS)


def solution(mesh):
    fine = Mesh(mesh.devices.reshape(16, 2, 2, 4, 2), ("z", "y_hi", "y_lo", "x", "core"))
    state = ("z", "y_hi")
    member = ("y_lo", "x", "core")
    placed = (
        P(state),
        P(member, state),
        P(member, None),
        P(member),
        P(state),
        P(state),
        P(state),
        P(),
    )
    return jax.shard_map(
        on_device,
        mesh=fine,
        in_specs=placed,
        out_specs=(P(member, state), P(member)),
        check_vma=False,
    )
```

```python
import math

import jax
import jax.numpy as jnp
from jax import lax
from jax.experimental import pallas as pl
from jax.experimental.pallas import tpu as pltpu
from jax.sharding import Mesh, PartitionSpec as P

M = 1024
S = 4096
REACH = 512
TAPS = 8
ROWS = 64
GROUP = 8
COLS = S // GROUP
CH = 256
PITCH = 80
BF = jnp.bfloat16
F32 = jnp.float32
NT = (((1,), (1,)), ((), ()))
VMEM_LIMIT = 50 * 1024 * 1024


def call(kernel, out_shape, in_specs, scratch=(), flops=0, nbytes=0):
    return pl.pallas_call(
        kernel,
        out_shape=out_shape,
        in_specs=in_specs,
        out_specs=jax.tree.map(lambda _: pl.BlockSpec(memory_space=pltpu.VMEM), out_shape),
        scratch_shapes=list(scratch),
        compiler_params=pltpu.CompilerParams(vmem_limit_bytes=VMEM_LIMIT),
        cost_estimate=pl.CostEstimate(flops=flops, bytes_accessed=nbytes, transcendentals=0),
    )


def vmem():
    return pl.BlockSpec(memory_space=pltpu.VMEM)


def smem():
    return pl.BlockSpec(memory_space=pltpu.SMEM)


def shape(*dims):
    return jax.ShapeDtypeStruct(dims, BF)


def shape32(*dims):
    return jax.ShapeDtypeStruct(dims, F32)


def three_parts(value):
    high = value.astype(BF)
    rest = value - high.astype(F32)
    middle = rest.astype(BF)
    low = (rest - middle.astype(F32)).astype(BF)
    return high, middle, low


def base_rows(base):
    high, middle, low = three_parts(base)
    zeros = jnp.zeros((13, base.shape[1]), BF)
    return jnp.concatenate([high, middle, low, zeros], axis=0)


def edge_kernel(anomalies, base, low, high, base_low, base_high, sems):
    first = pl.ds(0, REACH)
    last = pl.ds(S - REACH, REACH)
    copies = [
        pltpu.make_async_copy(anomalies.at[:, first], low.at[pl.ds(0, ROWS)], sems.at[0]),
        pltpu.make_async_copy(anomalies.at[:, last], high.at[pl.ds(0, ROWS)], sems.at[1]),
        pltpu.make_async_copy(base.at[:, first], base_low, sems.at[2]),
        pltpu.make_async_copy(base.at[:, last], base_high, sems.at[3]),
    ]
    for copy in copies:
        copy.start()
    for copy in copies:
        copy.wait()
    low[ROWS:] = base_rows(base_low[...])
    high[ROWS:] = base_rows(base_high[...])


def stencil_kernel(
    place, offsets, anomalies, base, below, above, transform, out, base_mean, rows, means
):
    def fill(chunk, block, extra):
        at = chunk * PITCH
        rows[at : at + ROWS] = block
        rows[at + ROWS : at + PITCH] = extra

    inner = S // CH
    outer = REACH // CH
    for k in range(outer):
        c = slice(k * CH, k * CH + CH)
        fill(k, below[0:ROWS, c], below[ROWS:, c])
        fill(outer + inner + k, above[0:ROWS, c], above[ROWS:, c])
    for k in range(inner):
        c = slice(k * CH, k * CH + CH)
        fill(outer + k, anomalies[:, c], base_rows(base[:, c]))

    total = jnp.zeros((inner * PITCH, CH), F32)
    for k in range(2 * outer + 1):
        shift = (
            lax.broadcasted_iota(jnp.int32, (CH, CH), 0)
            - lax.broadcasted_iota(jnp.int32, (CH, CH), 1)
            + (k * CH - REACH)
        )
        count = jnp.zeros((CH, CH), F32)
        for tap in range(TAPS):
            count = count + jnp.where(shift == offsets[tap], 1.0 / TAPS, 0.0)
        total = total + jnp.dot(
            rows[k * PITCH : (k + inner) * PITCH], count.astype(BF), preferred_element_type=F32
        )
    for k in range(inner):
        at = k * PITCH
        c = slice(k % 2 * CH, k % 2 * CH + CH)
        out[k // 2, :, c] = total[at : at + ROWS].astype(BF)
        at = at + ROWS
        means[:, k * CH : k * CH + CH] = (
            total[at : at + 1] + total[at + 1 : at + 2] + total[at + 2 : at + 3]
        )
    for k in range(GROUP):
        out[k, :, COLS:] = transform[...]
    base_mean[...] = means[:, pl.ds(pl.multiple_of(place[1] * COLS, COLS), COLS)]


def weight_kernel(place, observed, obs_scale, obs_rows, weight_row, value_row):
    scale = obs_scale[...]
    square = scale * scale
    value = square * observed[...]
    at = obs_rows[...] - place[2]
    high = at >> 7
    low = at & 127
    lanes = lax.broadcasted_iota(jnp.int32, (128, S), 0) == low
    lanes = jnp.where(lanes, 1.0, 0.0).astype(BF)
    blocks = lax.broadcasted_iota(jnp.int32, (8, S), 0) == high
    parts = []
    for term in (square, value):
        for part in three_parts(term):
            parts.append(jnp.where(blocks, part.astype(F32), 0.0))
    left = jnp.concatenate(parts, axis=0).astype(BF)
    sums = lax.dot_general(left, lanes, NT, preferred_element_type=F32)
    weight = sums[0:8] + sums[8:16] + sums[16:24]
    worth = sums[24:32] + sums[32:40] + sums[40:48]
    for k in range(COLS // 128):
        weight_row[:, k * 128 : k * 128 + 128] = weight[k : k + 1]
        value_row[:, k * 128 : k * 128 + 128] = worth[k : k + 1]


def two_part_rows(value, count):
    high = value.astype(BF).astype(F32)
    low = value - high
    row = jnp.concatenate([high, low], axis=1)
    return jnp.concatenate([row, jnp.zeros((count - 1, 128), F32)], axis=0).astype(BF)


def gram_kernel(
    place, mine, other, base_mean, weight_row, value_row,
    out, transform, gathered, centred, scaled, part,
):
    core = place[0]
    for k in range(GROUP):
        for block, side in ((mine, core), (other, 1 - core)):
            at = pl.ds(pl.multiple_of(k * 128 + side * ROWS, ROWS), ROWS)
            gathered[at] = block[k, :, 0:COLS]
            transform[at] = block[k, :, COLS:]

    own = [pl.ds(pl.multiple_of(k * 128 + core * ROWS, ROWS), ROWS) for k in range(GROUP)]
    for k in range(COLS // CH):
        c = slice(k * CH, k * CH + CH)
        mean = jnp.dot(transform[...], gathered[:, c], preferred_element_type=F32)
        mean = mean + base_mean[:, c]
        predicted = mean + 0.25 * mean * mean
        average = jnp.sum(predicted, axis=0, keepdims=True) * (1.0 / M)
        difference = predicted - average
        centred[k] = difference
        weight = weight_row[:, c]
        scaled[:, c] = (difference * jnp.sqrt(weight * (1.0 / (M - 1)))).astype(BF)
        slope = (value_row[:, c] - weight * average) * (1.0 / math.sqrt(M - 1))
        for j in range(GROUP):
            product = centred[k, own[j]] * slope
            product = product[:, :128] + product[:, 128:]
            if k == 0:
                part[j * ROWS : j * ROWS + ROWS] = product
            else:
                part[j * ROWS : j * ROWS + ROWS] += product
    rows = jnp.concatenate([scaled[own[j]] for j in range(GROUP)], axis=0)
    slopes = jnp.sum(part[...].T, axis=0, keepdims=True)
    left_half = lax.broadcasted_iota(jnp.int32, (16, 128), 1) < ROWS
    gram = lax.dot_general(scaled[...], rows, NT, preferred_element_type=F32)
    for j in range(GROUP):
        lanes = slice(j // 2 * 128, j // 2 * 128 + 128)
        tail = two_part_rows(slopes[:, j * ROWS : j * ROWS + ROWS], 16)
        for y_hi in range(2):
            target = out.at[y_hi * GROUP + j]
            for z in range(16):
                at = z * 64 + y_hi * 32
                top = gram[at : at + 16, lanes]
                bottom = gram[at + 16 : at + 32, lanes]
                if j % 2 == 0:
                    packed = jnp.where(left_half, top, pltpu.roll(bottom, ROWS, 1))
                else:
                    packed = jnp.where(left_half, pltpu.roll(top, ROWS, 1), bottom)
                target[z * 16 : z * 16 + 16] = packed.astype(BF)
            target[256:272] = tail


def middle_kernel(parts, out):
    total = jnp.sum(parts[...].astype(F32), axis=0)
    tail = two_part_rows(total[256:257, 0:ROWS] + total[256:257, ROWS:], 8)
    for z in range(16):
        out[z, 0:16] = total[z * 16 : z * 16 + 16].astype(BF)
        out[z, 16:24] = tail


def last_kernel(place, parts, weights, hessian, gradient):
    total = jnp.sum(parts[...].astype(F32), axis=0)
    packed = total[0:16]
    tall = jnp.concatenate([packed, jnp.zeros((112, 128), F32)], axis=0).T
    block = jnp.concatenate([tall[0:ROWS, 0:16], tall[ROWS:, 0:16]], axis=1)
    row = lax.broadcasted_iota(jnp.int32, (ROWS, 32), 0) + place[3]
    column = lax.broadcasted_iota(jnp.int32, (ROWS, 32), 1) + place[4]
    hessian[...] = block + jnp.where(row == column, 1.0, 0.0)
    gradient[...] = weights[...] - (total[16:17, 0:ROWS] + total[16:17, ROWS:])


def on_device(base_state, anomalies, transform, weights, observed, obs_scale, obs_rows, offsets):
    state = lax.axis_index("z") * 2 + lax.axis_index("y_hi")
    core = lax.axis_index("core")
    column = lax.axis_index("y_lo") * 4 + lax.axis_index("x")
    place = jnp.stack(
        [core, column, state * S + column * COLS, (column * 2 + core) * ROWS, state * 32]
    ).astype(jnp.int32)
    row = lambda v: v.reshape(1, S)

    low, high = call(
        edge_kernel,
        (shape(PITCH, REACH), shape(PITCH, REACH)),
        [pl.BlockSpec(memory_space=pl.ANY)] * 2,
        scratch=[
            pltpu.VMEM((1, REACH), F32),
            pltpu.VMEM((1, REACH), F32),
            pltpu.SemaphoreType.DMA((4,)),
        ],
        nbytes=2**18,
    )(anomalies, row(base_state))
    up = [(s, s + 1) for s in range(31)]
    down = [(s + 1, s) for s in range(31)]
    below = lax.ppermute(high, ("z", "y_hi"), up)
    above = lax.ppermute(low, ("z", "y_hi"), down)

    weight_row, value_row = call(
        weight_kernel,
        (shape32(1, COLS), shape32(1, COLS)),
        [smem(), vmem(), vmem(), vmem()],
        flops=2 * 48 * S * 128,
        nbytes=2**20,
    )(place, row(observed), row(obs_scale), row(obs_rows))

    outgoing, base_mean = call(
        stencil_kernel,
        (shape(GROUP, ROWS, COLS + M), shape32(1, COLS)),
        [smem(), smem()] + [vmem()] * 5,
        scratch=[
            pltpu.VMEM(((S + 2 * REACH) // CH * PITCH, CH), BF),
            pltpu.VMEM((1, S), F32),
        ],
        flops=2 * 1280 * 1280 * 256,
        nbytes=2**21,
    )(place, offsets, anomalies, row(base_state), below, above, transform)

    mine = lax.all_to_all(outgoing, ("y_lo", "x"), 0, 0)
    other = lax.ppermute(mine, "core", [(0, 1), (1, 0)])

    parts = call(
        gram_kernel,
        shape(2 * GROUP, 272, 128),
        [smem()] + [vmem()] * 5,
        scratch=[
            pltpu.VMEM((M, M), BF),
            pltpu.VMEM((M, COLS), BF),
            pltpu.VMEM((COLS // CH, M, CH), F32),
            pltpu.VMEM((M, COLS), BF),
            pltpu.VMEM((GROUP * ROWS, 128), F32),
        ],
        flops=2 * M * M * 768,
        nbytes=2**22,
    )(place, mine, other, base_mean, weight_row, value_row)
    parts = lax.all_to_all(parts, ("y_hi", "y_lo", "x"), 0, 0)
    sums = call(middle_kernel, shape(16, 24, 128), [vmem()], nbytes=2**20)(parts)
    sums = lax.all_to_all(sums, "z", 0, 0)
    hessian, gradient = call(
        last_kernel, (shape32(ROWS, 32), shape32(1, ROWS)), [smem(), vmem(), vmem()], nbytes=2**18
    )(place, sums, weights.reshape(1, ROWS))
    return hessian, gradient.reshape(ROWS)


def solution(mesh):
    fine = Mesh(mesh.devices.reshape(16, 2, 2, 4, 2), ("z", "y_hi", "y_lo", "x", "core"))
    state = ("z", "y_hi")
    member = ("y_lo", "x", "core")
    placed = (
        P(state),
        P(member, state),
        P(member, None),
        P(member),
        P(state),
        P(state),
        P(state),
        P(),
    )
    return jax.shard_map(
        on_device,
        mesh=fine,
        in_specs=placed,
        out_specs=(P(member, state), P(member)),
        check_vma=False,
    )
```

```python
import math

import jax
import jax.numpy as jnp
from jax import lax
from jax.experimental import pallas as pl
from jax.experimental.pallas import tpu as pltpu
from jax.sharding import Mesh, PartitionSpec as P

M = 1024
S = 4096
REACH = 512
TAPS = 8
ROWS = 64
GROUP = 8
COLS = S // GROUP
CH = 256
PITCH = 80
EDGE = 2 * REACH
TILES = 2 * REACH // CH + 1
OUTER = EDGE // CH
INNER = S // CH - OUTER
BF = jnp.bfloat16
F32 = jnp.float32
NT = (((1,), (1,)), ((), ()))
MIB = 2**20
FULL = 63


def call(kernel, out_shape, in_specs, scratch=(), flops=0, nbytes=0, limit=16, alias=None):
    return pl.pallas_call(
        kernel,
        out_shape=out_shape,
        in_specs=in_specs,
        out_specs=jax.tree.map(lambda _: pl.BlockSpec(memory_space=pltpu.VMEM), out_shape),
        scratch_shapes=list(scratch),
        compiler_params=pltpu.CompilerParams(vmem_limit_bytes=limit * MIB),
        input_output_aliases=alias or {},
        cost_estimate=pl.CostEstimate(flops=flops, bytes_accessed=nbytes, transcendentals=0),
    )


def spot():
    state = lax.axis_index("z") * 2 + lax.axis_index("y_hi")
    column = lax.axis_index("y_lo") * 4 + lax.axis_index("x")
    return state, column, (column * 2 + lax.axis_index("core")) * ROWS, state * 32


def vmem():
    return pl.BlockSpec(memory_space=pltpu.VMEM)


def smem():
    return pl.BlockSpec(memory_space=pltpu.SMEM)


def hbm():
    return pl.BlockSpec(memory_space=pltpu.HBM)


def shape(*dims):
    return jax.ShapeDtypeStruct(dims, BF)


def shape32(*dims):
    return jax.ShapeDtypeStruct(dims, F32)


def three_parts(value):
    high = value.astype(BF)
    rest = value - high.astype(F32)
    middle = rest.astype(BF)
    low = (rest - middle.astype(F32)).astype(BF)
    return high, middle, low


def base_rows(base):
    high, middle, low = three_parts(base)
    zeros = jnp.zeros((13, base.shape[1]), BF)
    return jnp.concatenate([high, middle, low, zeros], axis=0)


def sums_at_rows(first_line, lines, observed, obs_scale, at):
    square = obs_scale * obs_scale
    value = square * observed
    high = at >> 7
    low = at & 127
    lanes = lax.broadcasted_iota(jnp.int32, (128, S), 0) == low
    lanes = jnp.where(lanes, 1.0, 0.0).astype(BF)
    line = lax.broadcasted_iota(jnp.int32, (8, S), 0)
    blocks = (line + first_line == high) & (line < lines)
    parts = []
    for term in (square, value):
        for part in three_parts(term):
            parts.append(jnp.where(blocks, part.astype(F32), 0.0))
    left = jnp.concatenate(parts, axis=0).astype(BF)
    sums = lax.dot_general(left, lanes, NT, preferred_element_type=F32)
    weight = sums[0:8] + sums[8:16] + sums[16:24]
    value = sums[24:32] + sums[32:40] + sums[40:48]
    return [weight[k : k + 1] for k in range(lines)], [value[k : k + 1] for k in range(lines)]


def edge_kernel(
    anomalies, base, observed, obs_scale, obs_rows, edge,
    base_edge, observed_all, scale_all, rows_all, sems,
):
    border = pl.ds(S - EDGE, EDGE)
    copies = [
        pltpu.make_async_copy(obs_rows, rows_all, sems.at[0]),
        pltpu.make_async_copy(obs_scale, scale_all, sems.at[1]),
        pltpu.make_async_copy(observed, observed_all, sems.at[2]),
        pltpu.make_async_copy(base.at[:, border], base_edge, sems.at[3]),
        pltpu.make_async_copy(anomalies.at[:, border], edge.at[pl.ds(0, ROWS)], sems.at[4]),
    ]
    for copy in copies:
        copy.start()
    for copy in copies[:4]:
        copy.wait()
    weight, value = sums_at_rows(
        S // 128 - 4, 4, observed_all[...], scale_all[...], rows_all[...] - spot()[0] * S
    )
    empty = [jnp.zeros((1, EDGE - REACH), F32)]
    extra = list(three_parts(base_edge[...]))
    for row in (weight, value):
        extra += three_parts(jnp.concatenate(empty + row, axis=1))
    extra.append(jnp.zeros((7, EDGE), BF))
    edge[ROWS:] = jnp.concatenate(extra, axis=0)
    copies[4].wait()


def banded(rows, band, first, count):
    total = jnp.zeros((count * PITCH, CH), F32)
    for k in range(TILES):
        at = (first + k) * PITCH
        total = total + jnp.dot(
            rows[at : at + count * PITCH],
            band[k * CH : k * CH + CH],
            preferred_element_type=F32,
        )
    return total


def put_chunk(total, k, chunk, out, means):
    at = k * PITCH
    out[chunk // 2, :, chunk % 2 * CH : chunk % 2 * CH + CH] = total[at : at + ROWS].astype(BF)
    at = at + ROWS
    means[:, chunk * CH : chunk * CH + CH] = (
        total[at : at + 1] + total[at + 1 : at + 2] + total[at + 2 : at + 3]
    )


def inner_kernel(offsets, anomalies, base, transform, out, band, border, means, rows, sems):
    copies = [
        pltpu.make_async_copy(transform, out.at[k, :, pl.ds(COLS, M)], sems.at[k])
        for k in range(GROUP)
    ]
    for copy in copies:
        copy.start()
    for k in range(S // CH):
        c = slice(k * CH, k * CH + CH)
        at = k * PITCH
        rows[at : at + ROWS] = anomalies[:, c]
        rows[at + ROWS : at + PITCH] = base_rows(base[:, c])
    for k in range(TILES):
        shift = (
            lax.broadcasted_iota(jnp.int32, (CH, CH), 0)
            - lax.broadcasted_iota(jnp.int32, (CH, CH), 1)
            + (k * CH - REACH)
        )
        count = jnp.zeros((CH, CH), F32)
        for tap in range(TAPS):
            count = count + jnp.where(shift == offsets[tap], 1.0 / TAPS, 0.0)
        band[k * CH : k * CH + CH] = count.astype(BF)
    total = banded(rows, band, 0, INNER)
    means[...] = jnp.zeros_like(means)
    for k in range(INNER):
        put_chunk(total, k, k + OUTER, out, means)
    border[...] = rows[0 : OUTER * PITCH]
    for copy in copies:
        copy.wait()


def outer_kernel(edge, band, border, means_in, out_in, out, base_mean, rows, means):
    state, column, _, _ = spot()
    whole = state > 0
    means[...] = means_in[...]
    for k in range(OUTER):
        at = k * PITCH
        rows[at : at + PITCH] = edge[:, k * CH : k * CH + CH]
        rows[at + OUTER * PITCH : at + (OUTER + 1) * PITCH] = border[at : at + PITCH]
    seen = jnp.where(whole, 1.0, 0.0).astype(BF)
    before = rows[2 * PITCH : 4 * PITCH]
    after = rows[4 * PITCH : 6 * PITCH]
    rows[4 * PITCH : 6 * PITCH] = after * seen
    total = banded(rows, band, 0, 2)
    for k in range(2):
        put_chunk(total, k, k, out, means)
    rows[4 * PITCH : 6 * PITCH] = after
    rows[2 * PITCH : 4 * PITCH] = before * seen
    total = banded(rows, band, 2, 2)
    for k in range(2):
        put_chunk(total, k, k + 2, out, means)
    base_mean[...] = means[:, pl.ds(pl.multiple_of(column * COLS, COLS), COLS)]


def weight_kernel(observed, obs_scale, obs_rows, edge, weight_row, value_row):
    state, column, _, _ = spot()
    weight, value = sums_at_rows(
        (column - 1) * 4, 4, observed[...], obs_scale[...], obs_rows[...] - state * S
    )
    half = pl.ds(EDGE - REACH, REACH)
    row = lambda k: edge[ROWS : ROWS + 16, half][k : k + 1].astype(F32)
    mine = column > 0
    for rows, target, at in ((weight, weight_row, 3), (value, value_row, 6)):
        sent = row(at) + row(at + 1) + row(at + 2)
        target[...] = jnp.where(mine, jnp.concatenate(rows, axis=1), sent)


def two_part_rows(value, count):
    high = value.astype(BF).astype(F32)
    low = value - high
    row = jnp.concatenate([high, low], axis=1)
    return jnp.concatenate([row, jnp.zeros((count - 1, 128), F32)], axis=0).astype(BF)


def gram_kernel(
    mine, other, base_mean, weight_row, value_row,
    out, transform, gathered, centred, scaled, part,
):
    core = lax.axis_index("core")
    for k in range(GROUP):
        for block, side in ((mine, core), (other, 1 - core)):
            at = pl.ds(pl.multiple_of(k * 128 + side * ROWS, ROWS), ROWS)
            gathered[at] = block[k, :, 0:COLS]
            transform[at] = block[k, :, COLS:]

    own = [pl.ds(pl.multiple_of(k * 128 + core * ROWS, ROWS), ROWS) for k in range(GROUP)]
    for k in range(COLS // CH):
        c = slice(k * CH, k * CH + CH)
        mean = jnp.dot(transform[...], gathered[:, c], preferred_element_type=F32)
        mean = mean + base_mean[:, c]
        predicted = mean + 0.25 * mean * mean
        average = jnp.sum(predicted, axis=0, keepdims=True) * (1.0 / M)
        difference = predicted - average
        centred[k] = difference
        weight = weight_row[:, c]
        scaled[:, c] = (difference * jnp.sqrt(weight * (1.0 / (M - 1)))).astype(BF)
        slope = (value_row[:, c] - weight * average) * (1.0 / math.sqrt(M - 1))
        for j in range(GROUP):
            product = centred[k, own[j]] * slope
            product = product[:, :128] + product[:, 128:]
            if k == 0:
                part[j * ROWS : j * ROWS + ROWS] = product
            else:
                part[j * ROWS : j * ROWS + ROWS] += product
    rows = jnp.concatenate([scaled[own[j]] for j in range(GROUP)], axis=0)
    slopes = jnp.sum(part[...].T, axis=0, keepdims=True)
    left_half = lax.broadcasted_iota(jnp.int32, (16, 128), 1) < ROWS
    gram = lax.dot_general(scaled[...], rows, NT, preferred_element_type=F32)
    for j in range(GROUP):
        lanes = slice(j // 2 * 128, j // 2 * 128 + 128)
        tail = two_part_rows(slopes[:, j * ROWS : j * ROWS + ROWS], 16)
        for y_hi in range(2):
            target = out.at[y_hi * GROUP + j]
            for z in range(16):
                at = z * 64 + y_hi * 32
                top = gram[at : at + 16, lanes]
                bottom = gram[at + 16 : at + 32, lanes]
                if j % 2 == 0:
                    packed = jnp.where(left_half, top, pltpu.roll(bottom, ROWS, 1))
                else:
                    packed = jnp.where(left_half, pltpu.roll(top, ROWS, 1), bottom)
                target[z * 16 : z * 16 + 16] = packed.astype(BF)
            target[256:272] = tail


def middle_kernel(parts, out):
    total = jnp.sum(parts[...].astype(F32), axis=0)
    tail = two_part_rows(total[256:257, 0:ROWS] + total[256:257, ROWS:], 8)
    for z in range(16):
        out[z, 0:16] = total[z * 16 : z * 16 + 16].astype(BF)
        out[z, 16:24] = tail


def last_kernel(parts, weights, hessian, gradient):
    _, _, row0, column0 = spot()
    total = jnp.sum(parts[...].astype(F32), axis=0)
    row = lax.broadcasted_iota(jnp.int32, (16, ROWS), 1) + row0
    column = lax.broadcasted_iota(jnp.int32, (16, ROWS), 0) + column0
    for half in range(2):
        block = total[0:16, half * ROWS : half * ROWS + ROWS]
        same = row == column + half * 16
        hessian[half * 16 : half * 16 + 16] = block + jnp.where(same, 1.0, 0.0)
    gradient[...] = weights[...] - (total[16:17, 0:ROWS] + total[16:17, ROWS:])


def on_device(base_state, anomalies, transform, weights, observed, obs_scale, obs_rows, offsets):
    row = lambda v: v.reshape(1, S)
    base = row(base_state)
    obs = (row(observed), row(obs_scale), row(obs_rows))

    edge = call(
        edge_kernel,
        shape(PITCH, EDGE),
        [hbm()] * 5,
        scratch=[
            pltpu.VMEM((1, EDGE), F32),
            pltpu.VMEM((1, S), F32),
            pltpu.VMEM((1, S), F32),
            pltpu.VMEM((1, S), jnp.int32),
            pltpu.SemaphoreType.DMA((5,)),
        ],
        nbytes=MIB,
        limit=FULL,
    )(anomalies, base, *obs)
    edge = lax.ppermute(edge, ("z", "y_hi"), [(s, (s + 1) % 32) for s in range(32)])

    outgoing, band, border, means = call(
        inner_kernel,
        (
            shape(GROUP, ROWS, COLS + M),
            shape(TILES * CH, CH),
            shape(OUTER * PITCH, CH),
            shape32(1, S),
        ),
        [smem()] + [vmem()] * 2 + [hbm()],
        scratch=[
            pltpu.VMEM((S // CH * PITCH, CH), BF),
            pltpu.SemaphoreType.DMA((GROUP,)),
        ],
        flops=2 * INNER * PITCH * TILES * CH * CH,
        nbytes=4 * MIB,
    )(offsets, anomalies, base, transform)
    outgoing, base_mean = call(
        outer_kernel,
        (shape(GROUP, ROWS, COLS + M), shape32(1, COLS)),
        [vmem()] * 5,
        scratch=[pltpu.VMEM((2 * OUTER * PITCH, CH), BF), pltpu.VMEM((1, S), F32)],
        flops=2 * OUTER * PITCH * TILES * CH * CH,
        nbytes=MIB,
        alias={4: 0},
    )(edge, band, border, means, outgoing)

    mine = lax.all_to_all(outgoing, ("y_lo", "x"), 0, 0)
    other = lax.ppermute(mine, "core", [(0, 1), (1, 0)])

    weight_row, value_row = call(
        weight_kernel,
        (shape32(1, COLS), shape32(1, COLS)),
        [vmem()] * 4,
        flops=2 * 48 * S * 128,
        nbytes=MIB,
    )(*obs, edge)

    parts = call(
        gram_kernel,
        shape(2 * GROUP, 272, 128),
        [vmem()] * 5,
        scratch=[
            pltpu.VMEM((M, M), BF),
            pltpu.VMEM((M, COLS), BF),
            pltpu.VMEM((COLS // CH, M, CH), F32),
            pltpu.VMEM((M, COLS), BF),
            pltpu.VMEM((GROUP * ROWS, 128), F32),
        ],
        flops=2 * M * M * 768,
        nbytes=4 * MIB,
        limit=32,
    )(mine, other, base_mean, weight_row, value_row)
    parts = lax.all_to_all(parts, ("y_hi", "y_lo", "x"), 0, 0)
    sums = call(middle_kernel, shape(16, 24, 128), [vmem()], nbytes=2**20)(parts)
    sums = lax.all_to_all(sums, "z", 0, 0)
    hessian, gradient = call(
        last_kernel, (shape32(32, ROWS), shape32(1, ROWS)), [vmem()] * 2, nbytes=MIB // 4
    )(sums, weights.reshape(1, ROWS))
    return hessian.T, gradient.reshape(ROWS)


def solution(mesh):
    fine = Mesh(mesh.devices.reshape(16, 2, 2, 4, 2), ("z", "y_hi", "y_lo", "x", "core"))
    state = ("z", "y_hi")
    member = ("y_lo", "x", "core")
    placed = (
        P(state),
        P(member, state),
        P(member, None),
        P(member),
        P(state),
        P(state),
        P(state),
        P(),
    )
    return jax.shard_map(
        on_device,
        mesh=fine,
        in_specs=placed,
        out_specs=(P(member, state), P(member)),
        check_vma=False,
    )
```

```python
import math

import jax
import jax.numpy as jnp
from jax import lax
from jax.experimental import pallas as pl
from jax.experimental.pallas import tpu as pltpu
from jax.sharding import Mesh, PartitionSpec as P

M = 1024
S = 4096
REACH = 512
TAPS = 8
ROWS = 64
GROUP = 8
COLS = S // GROUP
CH = 256
PITCH = 80
EDGE = 2 * REACH
TILES = 2 * REACH // CH + 1
OUTER = EDGE // CH
INNER = S // CH - OUTER
BF = jnp.bfloat16
F32 = jnp.float32
NT = (((1,), (1,)), ((), ()))
MIB = 2**20
FULL = 63


def call(kernel, out_shape, in_specs, scratch=(), flops=0, nbytes=0, limit=16, alias=None):
    return pl.pallas_call(
        kernel,
        out_shape=out_shape,
        in_specs=in_specs,
        out_specs=jax.tree.map(lambda _: pl.BlockSpec(memory_space=pltpu.VMEM), out_shape),
        scratch_shapes=list(scratch),
        compiler_params=pltpu.CompilerParams(vmem_limit_bytes=limit * MIB),
        input_output_aliases=alias or {},
        cost_estimate=pl.CostEstimate(flops=flops, bytes_accessed=nbytes, transcendentals=0),
    )


def spot():
    state = lax.axis_index("z") * 2 + lax.axis_index("y_hi")
    column = lax.axis_index("y_lo") * 4 + lax.axis_index("x")
    return state, column, (column * 2 + lax.axis_index("core")) * ROWS, state * 32


def vmem():
    return pl.BlockSpec(memory_space=pltpu.VMEM)


def smem():
    return pl.BlockSpec(memory_space=pltpu.SMEM)


def hbm():
    return pl.BlockSpec(memory_space=pltpu.HBM)


def shape(*dims):
    return jax.ShapeDtypeStruct(dims, BF)


def shape32(*dims):
    return jax.ShapeDtypeStruct(dims, F32)


def three_parts(value):
    high = value.astype(BF)
    rest = value - high.astype(F32)
    middle = rest.astype(BF)
    low = (rest - middle.astype(F32)).astype(BF)
    return high, middle, low


def base_rows(base):
    high, middle, low = three_parts(base)
    zeros = jnp.zeros((13, base.shape[1]), BF)
    return jnp.concatenate([high, middle, low, zeros], axis=0)


def sums_at_rows(first_line, observed, obs_scale, at):
    square = obs_scale * obs_scale
    high = at >> 7
    low = at & 127
    lanes = lax.broadcasted_iota(jnp.int32, (128, S), 0) == low
    lanes = jnp.where(lanes, 1.0, 0.0).astype(BF)
    line = lax.broadcasted_iota(jnp.int32, (8, S), 0)
    term = jnp.where(line < 4, square, square * observed)
    term = jnp.where((line & 3) + first_line == high, term, 0.0)
    left = jnp.concatenate([part.astype(F32) for part in three_parts(term)], axis=0).astype(BF)
    sums = lax.dot_general(left, lanes, NT, preferred_element_type=F32)
    sums = sums[0:8] + sums[8:16] + sums[16:24]
    rows = [jnp.concatenate([sums[k : k + 1] for k in range(at, at + 4)], axis=1) for at in (0, 4)]
    return rows


def edge_kernel(
    anomalies, base, observed, obs_scale, obs_rows, edge, first,
    base_edge, observed_all, scale_all, rows_all, sems,
):
    border = pl.ds(S - EDGE, EDGE)
    copies = [
        pltpu.make_async_copy(obs_rows, rows_all, sems.at[0]),
        pltpu.make_async_copy(obs_scale, scale_all, sems.at[1]),
        pltpu.make_async_copy(observed, observed_all, sems.at[2]),
        pltpu.make_async_copy(base.at[:, border], base_edge, sems.at[3]),
        pltpu.make_async_copy(anomalies.at[:, border], edge.at[pl.ds(0, ROWS)], sems.at[4]),
        pltpu.make_async_copy(anomalies.at[:, pl.ds(0, EDGE)], first, sems.at[5]),
    ]
    for copy in copies:
        copy.start()
    for copy in copies[:4]:
        copy.wait()
    weight, value = sums_at_rows(
        S // 128 - 4, observed_all[...], scale_all[...], rows_all[...] - spot()[0] * S
    )
    empty = jnp.zeros((1, EDGE - REACH), F32)
    extra = list(three_parts(base_edge[...]))
    for row in (weight, value):
        extra += three_parts(jnp.concatenate([empty, row], axis=1))
    extra.append(jnp.zeros((7, EDGE), BF))
    edge[ROWS:] = jnp.concatenate(extra, axis=0)
    copies[4].wait()
    copies[5].wait()


def banded(rows, band, first, count):
    total = jnp.zeros((count * PITCH, CH), F32)
    for k in range(TILES):
        at = (first + k) * PITCH
        total = total + jnp.dot(
            rows[at : at + count * PITCH],
            band[k * CH : k * CH + CH],
            preferred_element_type=F32,
        )
    return total


def put_chunk(total, k, chunk, out, means):
    at = k * PITCH
    out[chunk // 2, :, chunk % 2 * CH : chunk % 2 * CH + CH] = total[at : at + ROWS].astype(BF)
    at = at + ROWS
    means[:, chunk * CH : chunk * CH + CH] = (
        total[at : at + 1] + total[at + 1 : at + 2] + total[at + 2 : at + 3]
    )


def inner_kernel(offsets, anomalies, base, transform, out, band, border, means, rows, sems):
    copies = [
        pltpu.make_async_copy(transform, out.at[k, :, pl.ds(COLS, M)], sems.at[k])
        for k in range(GROUP)
    ]
    for copy in copies:
        copy.start()
    for k in range(S // CH):
        c = slice(k * CH, k * CH + CH)
        at = k * PITCH
        rows[at : at + ROWS] = anomalies[:, c]
        rows[at + ROWS : at + PITCH] = base_rows(base[:, c])
    for k in range(TILES):
        shift = (
            lax.broadcasted_iota(jnp.int32, (CH, CH), 0)
            - lax.broadcasted_iota(jnp.int32, (CH, CH), 1)
            + (k * CH - REACH)
        )
        count = jnp.zeros((CH, CH), F32)
        for tap in range(TAPS):
            count = count + jnp.where(shift == offsets[tap], 1.0 / TAPS, 0.0)
        band[k * CH : k * CH + CH] = count.astype(BF)
    total = banded(rows, band, 0, INNER)
    means[...] = jnp.zeros_like(means)
    for k in range(INNER):
        put_chunk(total, k, k + OUTER, out, means)
    for k in range(OUTER):
        border[k * 16 : k * 16 + 16] = rows[k * PITCH + ROWS : (k + 1) * PITCH]
    for copy in copies:
        copy.wait()


def outer_kernel(edge, first, band, border, means_in, out_in, out, base_mean, rows, means):
    state, column, _, _ = spot()
    whole = state > 0
    means[...] = means_in[...]
    for k in range(OUTER):
        at = k * PITCH
        rows[at : at + PITCH] = edge[:, k * CH : k * CH + CH]
        at = at + OUTER * PITCH
        rows[at : at + ROWS] = first[:, k * CH : k * CH + CH]
        rows[at + ROWS : at + PITCH] = border[k * 16 : k * 16 + 16]
    seen = jnp.where(whole, 1.0, 0.0).astype(BF)
    before = rows[2 * PITCH : 4 * PITCH]
    after = rows[4 * PITCH : 6 * PITCH]
    rows[4 * PITCH : 6 * PITCH] = after * seen
    total = banded(rows, band, 0, 2)
    for k in range(2):
        put_chunk(total, k, k, out, means)
    rows[4 * PITCH : 6 * PITCH] = after
    rows[2 * PITCH : 4 * PITCH] = before * seen
    total = banded(rows, band, 2, 2)
    for k in range(2):
        put_chunk(total, k, k + 2, out, means)
    base_mean[...] = means[:, pl.ds(pl.multiple_of(column * COLS, COLS), COLS)]


def weight_kernel(observed, obs_scale, obs_rows, edge, weight_row, value_row):
    state, column, _, _ = spot()
    weight, value = sums_at_rows(
        (column - 1) * 4, observed[...], obs_scale[...], obs_rows[...] - state * S
    )
    half = pl.ds(EDGE - REACH, REACH)
    row = lambda k: edge[ROWS : ROWS + 16, half][k : k + 1].astype(F32)
    mine = column > 0
    for own, target, at in ((weight, weight_row, 3), (value, value_row, 6)):
        sent = row(at) + row(at + 1) + row(at + 2)
        target[...] = jnp.where(mine, own, sent)


def two_part_rows(value, count):
    high = value.astype(BF).astype(F32)
    low = value - high
    row = jnp.concatenate([high, low], axis=1)
    return jnp.concatenate([row, jnp.zeros((count - 1, 128), F32)], axis=0).astype(BF)


def gram_kernel(
    mine, other, base_mean, weight_row, value_row,
    out, transform, gathered, centred, scaled, part,
):
    core = lax.axis_index("core")
    crossed = jnp.where(spot()[1] * COLS < EDGE, GROUP // 2, 0)
    for k in range(GROUP):
        for block, side in ((mine, core), (other, 1 - core)):
            at = pl.ds(pl.multiple_of(k * 128 + side * ROWS, ROWS), ROWS)
            transform[at] = block[k, :, COLS:]
            home = lax.rem(k + crossed, GROUP) * 128 + side * ROWS
            gathered[pl.ds(pl.multiple_of(home, ROWS), ROWS)] = block[k, :, 0:COLS]

    own = [pl.ds(pl.multiple_of(k * 128 + core * ROWS, ROWS), ROWS) for k in range(GROUP)]
    for k in range(COLS // CH):
        c = slice(k * CH, k * CH + CH)
        mean = jnp.dot(transform[...], gathered[:, c], preferred_element_type=F32)
        mean = mean + base_mean[:, c]
        predicted = mean + 0.25 * mean * mean
        average = jnp.sum(predicted, axis=0, keepdims=True) * (1.0 / M)
        difference = predicted - average
        centred[k] = difference
        weight = weight_row[:, c]
        scaled[:, c] = (difference * jnp.sqrt(weight * (1.0 / (M - 1)))).astype(BF)
        slope = (value_row[:, c] - weight * average) * (1.0 / math.sqrt(M - 1))
        for j in range(GROUP):
            product = centred[k, own[j]] * slope
            product = product[:, :128] + product[:, 128:]
            if k == 0:
                part[j * ROWS : j * ROWS + ROWS] = product
            else:
                part[j * ROWS : j * ROWS + ROWS] += product
    rows = jnp.concatenate([scaled[own[j]] for j in range(GROUP)], axis=0)
    slopes = jnp.sum(part[...].T, axis=0, keepdims=True)
    left_half = lax.broadcasted_iota(jnp.int32, (16, 128), 1) < ROWS
    gram = lax.dot_general(scaled[...], rows, NT, preferred_element_type=F32)
    for j in range(GROUP):
        lanes = slice(j // 2 * 128, j // 2 * 128 + 128)
        tail = two_part_rows(slopes[:, j * ROWS : j * ROWS + ROWS], 16)
        for y_hi in range(2):
            target = out.at[y_hi * GROUP + j]
            for z in range(16):
                at = z * 64 + y_hi * 32
                top = gram[at : at + 16, lanes]
                bottom = gram[at + 16 : at + 32, lanes]
                if j % 2 == 0:
                    packed = jnp.where(left_half, top, pltpu.roll(bottom, ROWS, 1))
                else:
                    packed = jnp.where(left_half, pltpu.roll(top, ROWS, 1), bottom)
                target[z * 16 : z * 16 + 16] = packed.astype(BF)
            target[256:272] = tail


def middle_kernel(parts, out):
    total = jnp.sum(parts[...].astype(F32), axis=0)
    tail = two_part_rows(total[256:257, 0:ROWS] + total[256:257, ROWS:], 16)
    for z in range(16):
        out[z, 0:16] = total[z * 16 : z * 16 + 16].astype(BF)
        out[z, 16:32] = tail


def last_kernel(parts, weights, hessian, gradient):
    _, _, row0, column0 = spot()
    total = jnp.sum(parts[...].astype(F32), axis=0)
    row = lax.broadcasted_iota(jnp.int32, (16, ROWS), 1) + row0
    column = lax.broadcasted_iota(jnp.int32, (16, ROWS), 0) + column0
    for half in range(2):
        block = total[0:16, half * ROWS : half * ROWS + ROWS]
        same = row == column + half * 16
        hessian[half * 16 : half * 16 + 16] = block + jnp.where(same, 1.0, 0.0)
    gradient[...] = weights[...] - (total[16:17, 0:ROWS] + total[16:17, ROWS:])


def on_device(base_state, anomalies, transform, weights, observed, obs_scale, obs_rows, offsets):
    row = lambda v: v.reshape(1, S)
    base = row(base_state)
    obs = (row(observed), row(obs_scale), row(obs_rows))

    edge, first = call(
        edge_kernel,
        (shape(PITCH, EDGE), shape(ROWS, EDGE)),
        [hbm()] * 5,
        scratch=[
            pltpu.VMEM((1, EDGE), F32),
            pltpu.VMEM((1, S), F32),
            pltpu.VMEM((1, S), F32),
            pltpu.VMEM((1, S), jnp.int32),
            pltpu.SemaphoreType.DMA((6,)),
        ],
        flops=4 * 10**9,
        nbytes=MIB,
        limit=FULL,
    )(anomalies, base, *obs)
    onward = [(d, (d + 2) % 64 ^ 1) for d in range(64)]
    edge = lax.ppermute(edge, ("z", "y_hi", "y_lo"), onward)
    first = lax.ppermute(first, "y_lo", [(0, 1), (1, 0)])

    outgoing, band, border, means = call(
        inner_kernel,
        (
            shape(GROUP, ROWS, COLS + M),
            shape(TILES * CH, CH),
            shape(OUTER * 16, CH),
            shape32(1, S),
        ),
        [smem()] + [vmem()] * 2 + [hbm()],
        scratch=[
            pltpu.VMEM((S // CH * PITCH, CH), BF),
            pltpu.SemaphoreType.DMA((GROUP,)),
        ],
        flops=2 * INNER * PITCH * TILES * CH * CH,
        nbytes=4 * MIB,
    )(offsets, anomalies, base, transform)
    outgoing, base_mean = call(
        outer_kernel,
        (shape(GROUP, ROWS, COLS + M), shape32(1, COLS)),
        [vmem()] * 6,
        scratch=[pltpu.VMEM((2 * OUTER * PITCH, CH), BF), pltpu.VMEM((1, S), F32)],
        flops=2 * OUTER * PITCH * TILES * CH * CH,
        nbytes=MIB,
        alias={5: 0},
    )(edge, first, band, border, means, outgoing)

    mine = lax.all_to_all(outgoing, ("y_lo", "x"), 0, 0)
    other = lax.ppermute(mine, "core", [(0, 1), (1, 0)])

    weight_row, value_row = call(
        weight_kernel,
        (shape32(1, COLS), shape32(1, COLS)),
        [vmem()] * 4,
        flops=2 * 48 * S * 128,
        nbytes=MIB,
    )(*obs, edge)

    parts = call(
        gram_kernel,
        shape(2 * GROUP, 272, 128),
        [vmem()] * 5,
        scratch=[
            pltpu.VMEM((M, M), BF),
            pltpu.VMEM((M, COLS), BF),
            pltpu.VMEM((COLS // CH, M, CH), F32),
            pltpu.VMEM((M, COLS), BF),
            pltpu.VMEM((GROUP * ROWS, 128), F32),
        ],
        flops=2 * M * M * 768,
        nbytes=4 * MIB,
        limit=32,
    )(mine, other, base_mean, weight_row, value_row)
    parts = lax.all_to_all(parts, ("y_hi", "y_lo", "x"), 0, 0)
    sums = call(middle_kernel, shape(16, 32, 128), [vmem()], nbytes=2**20)(parts)
    sums = lax.all_to_all(sums, "z", 0, 0)
    hessian, gradient = call(
        last_kernel, (shape32(32, ROWS), shape32(1, ROWS)), [vmem()] * 2, nbytes=MIB // 4
    )(sums, weights.reshape(1, ROWS))
    return hessian.T, gradient.reshape(ROWS)


def solution(mesh):
    fine = Mesh(mesh.devices.reshape(16, 2, 2, 4, 2), ("z", "y_hi", "y_lo", "x", "core"))
    state = ("z", "y_hi")
    member = ("y_lo", "x", "core")
    placed = (
        P(state),
        P(member, state),
        P(member, None),
        P(member),
        P(state),
        P(state),
        P(state),
        P(),
    )
    return jax.shard_map(
        on_device,
        mesh=fine,
        in_specs=placed,
        out_specs=(P(member, state), P(member)),
        check_vma=False,
    )
```

```python
import math

import jax
import jax.numpy as jnp
from jax import lax
from jax.experimental import pallas as pl
from jax.experimental.pallas import tpu as pltpu
from jax.sharding import Mesh, PartitionSpec as P

M = 1024
S = 4096
REACH = 512
TAPS = 8
ROWS = 64
GROUP = 8
COLS = S // GROUP
CH = 256
PITCH = 80
EDGE = 2 * REACH
TILES = 2 * REACH // CH + 1
OUTER = EDGE // CH
INNER = S // CH - OUTER
BF = jnp.bfloat16
F32 = jnp.float32
NT = (((1,), (1,)), ((), ()))
MIB = 2**20
FULL = 63


def call(
    kernel, out_shape, in_specs, scratch=(), flops=0, nbytes=0, limit=16, alias=None, out_specs=None
):
    return pl.pallas_call(
        kernel,
        out_shape=out_shape,
        in_specs=in_specs,
        out_specs=out_specs
        or jax.tree.map(lambda _: pl.BlockSpec(memory_space=pltpu.VMEM), out_shape),
        scratch_shapes=list(scratch),
        compiler_params=pltpu.CompilerParams(vmem_limit_bytes=limit * MIB),
        input_output_aliases=alias or {},
        cost_estimate=pl.CostEstimate(flops=flops, bytes_accessed=nbytes, transcendentals=0),
    )


def spot():
    state = lax.axis_index("z") * 2 + lax.axis_index("y_hi")
    column = lax.axis_index("y_lo") * 4 + lax.axis_index("x")
    return state, column, (column * 2 + lax.axis_index("core")) * ROWS, state * 32


def vmem():
    return pl.BlockSpec(memory_space=pltpu.VMEM)


def smem():
    return pl.BlockSpec(memory_space=pltpu.SMEM)


def hbm():
    return pl.BlockSpec(memory_space=pltpu.HBM)


def shape(*dims):
    return jax.ShapeDtypeStruct(dims, BF)


def shape32(*dims):
    return jax.ShapeDtypeStruct(dims, F32)


def three_parts(value):
    high = value.astype(BF)
    rest = value - high.astype(F32)
    middle = rest.astype(BF)
    low = (rest - middle.astype(F32)).astype(BF)
    return high, middle, low


def base_rows(base):
    high, middle, low = three_parts(base)
    zeros = jnp.zeros((13, base.shape[1]), BF)
    return jnp.concatenate([high, middle, low, zeros], axis=0)


def sums_at_rows(first_line, observed, obs_scale, at):
    square = obs_scale * obs_scale
    high = at >> 7
    low = at & 127
    lanes = lax.broadcasted_iota(jnp.int32, (128, S), 0) == low
    lanes = jnp.where(lanes, 1.0, 0.0).astype(BF)
    line = lax.broadcasted_iota(jnp.int32, (8, S), 0)
    term = jnp.where(line < 4, square, square * observed)
    term = jnp.where((line & 3) + first_line == high, term, 0.0)
    left = jnp.concatenate([part.astype(F32) for part in three_parts(term)], axis=0).astype(BF)
    sums = lax.dot_general(left, lanes, NT, preferred_element_type=F32)
    sums = sums[0:8] + sums[8:16] + sums[16:24]
    rows = [jnp.concatenate([sums[k : k + 1] for k in range(at, at + 4)], axis=1) for at in (0, 4)]
    return rows


def edge_kernel(
    anomalies, base, observed, obs_scale, obs_rows, edge, first,
    base_edge, observed_all, scale_all, rows_all, sems,
):
    border = pl.ds(S - EDGE, EDGE)
    copies = [
        pltpu.make_async_copy(obs_rows, rows_all, sems.at[0]),
        pltpu.make_async_copy(obs_scale, scale_all, sems.at[1]),
        pltpu.make_async_copy(observed, observed_all, sems.at[2]),
        pltpu.make_async_copy(base.at[:, border], base_edge, sems.at[3]),
        pltpu.make_async_copy(anomalies.at[:, border], edge.at[pl.ds(0, ROWS)], sems.at[4]),
        pltpu.make_async_copy(anomalies.at[:, pl.ds(0, EDGE)], first, sems.at[5]),
    ]
    for copy in copies:
        copy.start()
    for copy in copies[:4]:
        copy.wait()
    weight, value = sums_at_rows(
        S // 128 - 4, observed_all[...], scale_all[...], rows_all[...] - spot()[0] * S
    )
    empty = jnp.zeros((1, EDGE - REACH), F32)
    extra = list(three_parts(base_edge[...]))
    for row in (weight, value):
        extra += three_parts(jnp.concatenate([empty, row], axis=1))
    extra.append(jnp.zeros((7, EDGE), BF))
    edge[ROWS:] = jnp.concatenate(extra, axis=0)
    copies[4].wait()
    copies[5].wait()


def banded(rows, band, first, count):
    total = jnp.zeros((count * PITCH, CH), F32)
    for k in range(TILES):
        at = (first + k) * PITCH
        total = total + jnp.dot(
            rows[at : at + count * PITCH],
            band[k * CH : k * CH + CH],
            preferred_element_type=F32,
        )
    return total


def put_chunk(total, k, chunk, out, means):
    at = k * PITCH
    out[chunk // 2, :, chunk % 2 * CH : chunk % 2 * CH + CH] = total[at : at + ROWS].astype(BF)
    at = at + ROWS
    means[:, chunk * CH : chunk * CH + CH] = (
        total[at : at + 1] + total[at + 1 : at + 2] + total[at + 2 : at + 3]
    )


def inner_kernel(offsets, anomalies, base, transform, out, band, border, means, rows, sems):
    copies = [
        pltpu.make_async_copy(transform, out.at[k, :, pl.ds(COLS, M)], sems.at[k])
        for k in range(GROUP)
    ]
    for copy in copies:
        copy.start()
    for k in range(S // CH):
        c = slice(k * CH, k * CH + CH)
        at = k * PITCH
        rows[at : at + ROWS] = anomalies[:, c]
        rows[at + ROWS : at + PITCH] = base_rows(base[:, c])
    for k in range(TILES):
        shift = (
            lax.broadcasted_iota(jnp.int32, (CH, CH), 0)
            - lax.broadcasted_iota(jnp.int32, (CH, CH), 1)
            + (k * CH - REACH)
        )
        count = jnp.zeros((CH, CH), F32)
        for tap in range(TAPS):
            count = count + jnp.where(shift == offsets[tap], 1.0 / TAPS, 0.0)
        band[k * CH : k * CH + CH] = count.astype(BF)
    total = banded(rows, band, 0, INNER)
    means[...] = jnp.zeros_like(means)
    for k in range(INNER):
        put_chunk(total, k, k + OUTER, out, means)
    for k in range(OUTER):
        border[k * 16 : k * 16 + 16] = rows[k * PITCH + ROWS : (k + 1) * PITCH]
    for copy in copies:
        copy.wait()


def outer_kernel(
    edge, first, band, border, means_in, out_in, out, base_mean, rows, means, chunks, sems
):
    state, column, _, _ = spot()
    whole = state > 0
    means[...] = means_in[...]
    for k in range(OUTER):
        at = k * PITCH
        rows[at : at + PITCH] = edge[:, k * CH : k * CH + CH]
        at = at + OUTER * PITCH
        rows[at : at + ROWS] = first[:, k * CH : k * CH + CH]
        rows[at + ROWS : at + PITCH] = border[k * 16 : k * 16 + 16]
    seen = jnp.where(whole, 1.0, 0.0).astype(BF)
    before = rows[2 * PITCH : 4 * PITCH]
    after = rows[4 * PITCH : 6 * PITCH]
    rows[4 * PITCH : 6 * PITCH] = after * seen
    total = banded(rows, band, 0, 2)
    for k in range(2):
        put_chunk(total, k, k, chunks, means)
    rows[4 * PITCH : 6 * PITCH] = after
    rows[2 * PITCH : 4 * PITCH] = before * seen
    total = banded(rows, band, 2, 2)
    for k in range(2):
        put_chunk(total, k, k + 2, chunks, means)
    copies = [
        pltpu.make_async_copy(chunks.at[k], out.at[k, :, pl.ds(0, COLS)], sems.at[k])
        for k in range(2)
    ]
    for copy in copies:
        copy.start()
    for copy in copies:
        copy.wait()
    base_mean[...] = means[:, pl.ds(pl.multiple_of(column * COLS, COLS), COLS)]


def weight_kernel(observed, obs_scale, obs_rows, edge, weight_row, value_row):
    state, column, _, _ = spot()
    weight, value = sums_at_rows(
        (column - 1) * 4, observed[...], obs_scale[...], obs_rows[...] - state * S
    )
    half = pl.ds(EDGE - REACH, REACH)
    row = lambda k: edge[ROWS : ROWS + 16, half][k : k + 1].astype(F32)
    mine = column > 0
    for own, target, at in ((weight, weight_row, 3), (value, value_row, 6)):
        sent = row(at) + row(at + 1) + row(at + 2)
        target[...] = jnp.where(mine, own, sent)


def two_part_rows(value, count):
    high = value.astype(BF).astype(F32)
    low = value - high
    row = jnp.concatenate([high, low], axis=1)
    return jnp.concatenate([row, jnp.zeros((count - 1, 128), F32)], axis=0).astype(BF)


def gram_kernel(
    mine, other, base_mean, weight_row, value_row,
    out, transform, gathered, centred, scaled, part,
):
    core = lax.axis_index("core")
    crossed = jnp.where(spot()[1] * COLS < EDGE, GROUP // 2, 0)
    for k in range(GROUP):
        for block, side in ((mine, core), (other, 1 - core)):
            at = pl.ds(pl.multiple_of(k * 128 + side * ROWS, ROWS), ROWS)
            transform[at] = block[k, :, COLS:]
            home = lax.rem(k + crossed, GROUP) * 128 + side * ROWS
            gathered[pl.ds(pl.multiple_of(home, ROWS), ROWS)] = block[k, :, 0:COLS]

    own = [pl.ds(pl.multiple_of(k * 128 + core * ROWS, ROWS), ROWS) for k in range(GROUP)]
    for k in range(COLS // CH):
        c = slice(k * CH, k * CH + CH)
        mean = jnp.dot(transform[...], gathered[:, c], preferred_element_type=F32)
        mean = mean + base_mean[:, c]
        predicted = mean + 0.25 * mean * mean
        average = jnp.sum(predicted, axis=0, keepdims=True) * (1.0 / M)
        difference = predicted - average
        centred[k] = difference
        weight = weight_row[:, c]
        scaled[:, c] = (difference * jnp.sqrt(weight * (1.0 / (M - 1)))).astype(BF)
        slope = (value_row[:, c] - weight * average) * (1.0 / math.sqrt(M - 1))
        for j in range(GROUP):
            product = centred[k, own[j]] * slope
            product = product[:, :128] + product[:, 128:]
            if k == 0:
                part[j * ROWS : j * ROWS + ROWS] = product
            else:
                part[j * ROWS : j * ROWS + ROWS] += product
    rows = jnp.concatenate([scaled[own[j]] for j in range(GROUP)], axis=0)
    slopes = jnp.sum(part[...].T, axis=0, keepdims=True)
    left_half = lax.broadcasted_iota(jnp.int32, (16, 128), 1) < ROWS
    gram = lax.dot_general(scaled[...], rows, NT, preferred_element_type=F32)
    for j in range(GROUP):
        lanes = slice(j // 2 * 128, j // 2 * 128 + 128)
        tail = two_part_rows(slopes[:, j * ROWS : j * ROWS + ROWS], 16)
        for y_hi in range(2):
            target = out.at[y_hi * GROUP + j]
            for z in range(16):
                at = z * 64 + y_hi * 32
                top = gram[at : at + 16, lanes]
                bottom = gram[at + 16 : at + 32, lanes]
                if j % 2 == 0:
                    packed = jnp.where(left_half, top, pltpu.roll(bottom, ROWS, 1))
                else:
                    packed = jnp.where(left_half, pltpu.roll(top, ROWS, 1), bottom)
                target[z * 16 : z * 16 + 16] = packed.astype(BF)
            target[256:272] = tail


def middle_kernel(parts, out):
    total = jnp.sum(parts[...].astype(F32), axis=0)
    tail = two_part_rows(total[256:257, 0:ROWS] + total[256:257, ROWS:], 16)
    for z in range(16):
        out[z, 0:16] = total[z * 16 : z * 16 + 16].astype(BF)
        out[z, 16:32] = tail


def last_kernel(parts, weights, hessian, gradient):
    _, _, row0, column0 = spot()
    total = jnp.sum(parts[...].astype(F32), axis=0)
    row = lax.broadcasted_iota(jnp.int32, (16, ROWS), 1) + row0
    column = lax.broadcasted_iota(jnp.int32, (16, ROWS), 0) + column0
    for half in range(2):
        block = total[0:16, half * ROWS : half * ROWS + ROWS]
        same = row == column + half * 16
        hessian[half * 16 : half * 16 + 16] = block + jnp.where(same, 1.0, 0.0)
    gradient[...] = weights[...] - (total[16:17, 0:ROWS] + total[16:17, ROWS:])


def on_device(base_state, anomalies, transform, weights, observed, obs_scale, obs_rows, offsets):
    row = lambda v: v.reshape(1, S)
    base = row(base_state)
    obs = (row(observed), row(obs_scale), row(obs_rows))

    edge, first = call(
        edge_kernel,
        (shape(PITCH, EDGE), shape(ROWS, EDGE)),
        [hbm()] * 5,
        scratch=[
            pltpu.VMEM((1, EDGE), F32),
            pltpu.VMEM((1, S), F32),
            pltpu.VMEM((1, S), F32),
            pltpu.VMEM((1, S), jnp.int32),
            pltpu.SemaphoreType.DMA((6,)),
        ],
        flops=4 * 10**9,
        nbytes=MIB,
        limit=FULL,
    )(anomalies, base, *obs)
    onward = [(d, (d + 2) % 64 ^ 1) for d in range(64)]
    edge = lax.ppermute(edge, ("z", "y_hi", "y_lo"), onward)
    first = lax.ppermute(first, "y_lo", [(0, 1), (1, 0)])

    outgoing, band, border, means = call(
        inner_kernel,
        (
            shape(GROUP, ROWS, COLS + M),
            shape(TILES * CH, CH),
            shape(OUTER * 16, CH),
            shape32(1, S),
        ),
        [smem()] + [vmem()] * 2 + [hbm()],
        scratch=[
            pltpu.VMEM((S // CH * PITCH, CH), BF),
            pltpu.SemaphoreType.DMA((GROUP,)),
        ],
        flops=2 * INNER * PITCH * TILES * CH * CH,
        nbytes=4 * MIB,
    )(offsets, anomalies, base, transform)
    anywhere = pl.BlockSpec(memory_space=pl.ANY)
    outgoing, base_mean = call(
        outer_kernel,
        (shape(GROUP, ROWS, COLS + M), shape32(1, COLS)),
        [vmem()] * 5 + [anywhere],
        scratch=[
            pltpu.VMEM((2 * OUTER * PITCH, CH), BF),
            pltpu.VMEM((1, S), F32),
            pltpu.VMEM((2, ROWS, COLS), BF),
            pltpu.SemaphoreType.DMA((2,)),
        ],
        flops=2 * OUTER * PITCH * TILES * CH * CH,
        nbytes=MIB,
        alias={5: 0},
        out_specs=(anywhere, vmem()),
    )(edge, first, band, border, means, outgoing)

    mine = lax.all_to_all(outgoing, ("y_lo", "x"), 0, 0)
    other = lax.ppermute(mine, "core", [(0, 1), (1, 0)])

    weight_row, value_row = call(
        weight_kernel,
        (shape32(1, COLS), shape32(1, COLS)),
        [vmem()] * 4,
        flops=2 * 48 * S * 128,
        nbytes=MIB,
    )(*obs, edge)

    parts = call(
        gram_kernel,
        shape(2 * GROUP, 272, 128),
        [vmem()] * 5,
        scratch=[
            pltpu.VMEM((M, M), BF),
            pltpu.VMEM((M, COLS), BF),
            pltpu.VMEM((COLS // CH, M, CH), F32),
            pltpu.VMEM((M, COLS), BF),
            pltpu.VMEM((GROUP * ROWS, 128), F32),
        ],
        flops=2 * M * M * 768,
        nbytes=4 * MIB,
        limit=32,
    )(mine, other, base_mean, weight_row, value_row)
    parts = lax.all_to_all(parts, ("y_hi", "y_lo", "x"), 0, 0)
    sums = call(middle_kernel, shape(16, 32, 128), [vmem()], nbytes=2**20)(parts)
    sums = lax.all_to_all(sums, "z", 0, 0)
    hessian, gradient = call(
        last_kernel, (shape32(32, ROWS), shape32(1, ROWS)), [vmem()] * 2, nbytes=MIB // 4
    )(sums, weights.reshape(1, ROWS))
    return hessian.T, gradient.reshape(ROWS)


def solution(mesh):
    fine = Mesh(mesh.devices.reshape(16, 2, 2, 4, 2), ("z", "y_hi", "y_lo", "x", "core"))
    state = ("z", "y_hi")
    member = ("y_lo", "x", "core")
    placed = (
        P(state),
        P(member, state),
        P(member, None),
        P(member),
        P(state),
        P(state),
        P(state),
        P(),
    )
    return jax.shard_map(
        on_device,
        mesh=fine,
        in_specs=placed,
        out_specs=(P(member, state), P(member)),
        check_vma=False,
    )
```

```python
import math

import jax
import jax.numpy as jnp
from jax import lax
from jax.experimental import pallas as pl
from jax.experimental.pallas import tpu as pltpu
from jax.sharding import Mesh, PartitionSpec as P

M = 1024
S = 4096
REACH = 512
TAPS = 8
ROWS = 64
GROUP = 8
COLS = S // GROUP
CH = 256
PITCH = 80
EDGE = 2 * REACH
TILES = 2 * REACH // CH + 1
OUTER = EDGE // CH
INNER = S // CH - OUTER
BF = jnp.bfloat16
F32 = jnp.float32
NT = (((1,), (1,)), ((), ()))
MIB = 2**20
FULL = 63


def call(
    kernel, out_shape, in_specs, scratch=(), flops=0, nbytes=0, limit=16, alias=None, out_specs=None
):
    return pl.pallas_call(
        kernel,
        out_shape=out_shape,
        in_specs=in_specs,
        out_specs=out_specs
        or jax.tree.map(lambda _: pl.BlockSpec(memory_space=pltpu.VMEM), out_shape),
        scratch_shapes=list(scratch),
        compiler_params=pltpu.CompilerParams(vmem_limit_bytes=limit * MIB),
        input_output_aliases=alias or {},
        cost_estimate=pl.CostEstimate(flops=flops, bytes_accessed=nbytes, transcendentals=0),
    )


def spot():
    state = lax.axis_index("z") * 2 + lax.axis_index("y_hi")
    column = lax.axis_index("y_lo") * 4 + lax.axis_index("x")
    return state, column, (column * 2 + lax.axis_index("core")) * ROWS, state * 32


def vmem():
    return pl.BlockSpec(memory_space=pltpu.VMEM)


def smem():
    return pl.BlockSpec(memory_space=pltpu.SMEM)


def hbm():
    return pl.BlockSpec(memory_space=pltpu.HBM)


def shape(*dims):
    return jax.ShapeDtypeStruct(dims, BF)


def shape32(*dims):
    return jax.ShapeDtypeStruct(dims, F32)


def three_parts(value):
    high = value.astype(BF)
    rest = value - high.astype(F32)
    middle = rest.astype(BF)
    low = (rest - middle.astype(F32)).astype(BF)
    return high, middle, low


def base_rows(base):
    high, middle, low = three_parts(base)
    zeros = jnp.zeros((13, base.shape[1]), BF)
    return jnp.concatenate([high, middle, low, zeros], axis=0)


def sums_at_rows(first_line, observed, obs_scale, at):
    square = obs_scale * obs_scale
    high = at >> 7
    low = at & 127
    lanes = lax.broadcasted_iota(jnp.int32, (128, S), 0) == low
    lanes = jnp.where(lanes, 1.0, 0.0).astype(BF)
    line = lax.broadcasted_iota(jnp.int32, (8, S), 0)
    term = jnp.where(line < 4, square, square * observed)
    term = jnp.where((line & 3) + first_line == high, term, 0.0)
    left = jnp.concatenate([part.astype(F32) for part in three_parts(term)], axis=0).astype(BF)
    sums = lax.dot_general(left, lanes, NT, preferred_element_type=F32)
    sums = sums[0:8] + sums[8:16] + sums[16:24]
    rows = [jnp.concatenate([sums[k : k + 1] for k in range(at, at + 4)], axis=1) for at in (0, 4)]
    return rows


def edge_kernel(
    anomalies, base, observed, obs_scale, obs_rows, edge, first,
    base_edge, observed_all, scale_all, rows_all, sems,
):
    border = pl.ds(S - EDGE, EDGE)
    copies = [
        pltpu.make_async_copy(obs_rows, rows_all, sems.at[0]),
        pltpu.make_async_copy(obs_scale, scale_all, sems.at[1]),
        pltpu.make_async_copy(observed, observed_all, sems.at[2]),
        pltpu.make_async_copy(base.at[:, border], base_edge, sems.at[3]),
        pltpu.make_async_copy(anomalies.at[:, border], edge.at[pl.ds(0, ROWS)], sems.at[4]),
        pltpu.make_async_copy(anomalies.at[:, pl.ds(0, EDGE)], first, sems.at[5]),
    ]
    for copy in copies:
        copy.start()
    for copy in copies[:4]:
        copy.wait()
    weight, value = sums_at_rows(
        S // 128 - 4, observed_all[...], scale_all[...], rows_all[...] - spot()[0] * S
    )
    empty = jnp.zeros((1, EDGE - REACH), F32)
    extra = list(three_parts(base_edge[...]))
    for row in (weight, value):
        extra += three_parts(jnp.concatenate([empty, row], axis=1))
    extra.append(jnp.zeros((7, EDGE), BF))
    edge[ROWS:] = jnp.concatenate(extra, axis=0)
    copies[4].wait()
    copies[5].wait()


def banded(rows, band, first, count):
    total = jnp.zeros((count * PITCH, CH), F32)
    for k in range(TILES):
        at = (first + k) * PITCH
        total = total + jnp.dot(
            rows[at : at + count * PITCH],
            band[k * CH : k * CH + CH],
            preferred_element_type=F32,
        )
    return total


def put_chunk(total, k, chunk, out, means):
    at = k * PITCH
    out[chunk // 2, :, chunk % 2 * CH : chunk % 2 * CH + CH] = total[at : at + ROWS].astype(BF)
    at = at + ROWS
    means[:, chunk * CH : chunk * CH + CH] = (
        total[at : at + 1] + total[at + 1 : at + 2] + total[at + 2 : at + 3]
    )


def inner_kernel(offsets, anomalies, base, transform, out, band, border, means, rows, sems):
    copies = [
        pltpu.make_async_copy(transform, out.at[k, :, pl.ds(COLS, M)], sems.at[k])
        for k in range(GROUP)
    ]
    for copy in copies:
        copy.start()
    for k in range(S // CH):
        c = slice(k * CH, k * CH + CH)
        at = k * PITCH
        rows[at : at + ROWS] = anomalies[:, c]
        rows[at + ROWS : at + PITCH] = base_rows(base[:, c])
    for k in range(TILES):
        shift = (
            lax.broadcasted_iota(jnp.int32, (CH, CH), 0)
            - lax.broadcasted_iota(jnp.int32, (CH, CH), 1)
            + (k * CH - REACH)
        )
        count = jnp.zeros((CH, CH), F32)
        for tap in range(TAPS):
            count = count + jnp.where(shift == offsets[tap], 1.0 / TAPS, 0.0)
        band[k * CH : k * CH + CH] = count.astype(BF)
    total = banded(rows, band, 0, INNER)
    means[...] = jnp.zeros_like(means)
    for k in range(INNER):
        put_chunk(total, k, k + OUTER, out, means)
    for k in range(OUTER):
        border[k * 16 : k * 16 + 16] = rows[k * PITCH + ROWS : (k + 1) * PITCH]
    for copy in copies:
        copy.wait()


def outer_kernel(
    edge, first, band, border, means_in, out_in, out, base_mean, rows, means, chunks, sems
):
    state, column, _, _ = spot()
    whole = state > 0
    means[...] = means_in[...]
    for k in range(OUTER):
        at = k * PITCH
        rows[at : at + PITCH] = edge[:, k * CH : k * CH + CH]
        at = at + OUTER * PITCH
        rows[at : at + ROWS] = first[:, k * CH : k * CH + CH]
        rows[at + ROWS : at + PITCH] = border[k * 16 : k * 16 + 16]
    seen = jnp.where(whole, 1.0, 0.0).astype(BF)
    before = rows[2 * PITCH : 4 * PITCH]
    after = rows[4 * PITCH : 6 * PITCH]
    rows[4 * PITCH : 6 * PITCH] = after * seen
    total = banded(rows, band, 0, 2)
    for k in range(2):
        put_chunk(total, k, k, chunks, means)
    rows[4 * PITCH : 6 * PITCH] = after
    rows[2 * PITCH : 4 * PITCH] = before * seen
    total = banded(rows, band, 2, 2)
    for k in range(2):
        put_chunk(total, k, k + 2, chunks, means)
    copies = [
        pltpu.make_async_copy(chunks.at[k], out.at[k, :, pl.ds(0, COLS)], sems.at[k])
        for k in range(2)
    ]
    for copy in copies:
        copy.start()
    for copy in copies:
        copy.wait()
    base_mean[...] = means[:, pl.ds(pl.multiple_of(column * COLS, COLS), COLS)]


def weight_kernel(observed, obs_scale, obs_rows, edge, weight_row, value_row):
    state, column, _, _ = spot()
    weight, value = sums_at_rows(
        (column - 1) * 4, observed[...], obs_scale[...], obs_rows[...] - state * S
    )
    half = pl.ds(EDGE - REACH, REACH)
    row = lambda k: edge[ROWS : ROWS + 16, half][k : k + 1].astype(F32)
    mine = column > 0
    for own, target, at in ((weight, weight_row, 3), (value, value_row, 6)):
        sent = row(at) + row(at + 1) + row(at + 2)
        target[...] = jnp.where(mine, own, sent)


def two_part_rows(value, count):
    high = value.astype(BF).astype(F32)
    low = value - high
    row = jnp.concatenate([high, low], axis=1)
    return jnp.concatenate([row, jnp.zeros((count - 1, 128), F32)], axis=0).astype(BF)


def seated_lanes(y_hi):
    lane = lax.broadcasted_iota(jnp.int32, (16, 128), 1)
    return (lane >= 16 + 32 * y_hi) & (lane < 24 + 32 * y_hi)


def seated(slopes):
    lane = lax.broadcasted_iota(jnp.int32, (16, 128), 1)
    mine = ((lane & (ROWS - 1)) >> 2) == lax.broadcasted_iota(jnp.int32, (16, 128), 0)
    high = slopes.astype(BF).astype(F32)
    low = slopes - high
    spread = []
    for j in range(GROUP):
        c = slice(j * ROWS, j * ROWS + ROWS)
        row = jnp.concatenate([high[:, c], low[:, c]], axis=1)
        spread.append(jnp.where(mine, row, 0.0))
    source = lax.broadcasted_iota(jnp.int32, (128, 128), 0)
    target = 16 + (source & 3) + jnp.where(source >= ROWS, 4, 0)
    pick = lax.broadcasted_iota(jnp.int32, (128, 128), 1) == target
    pick = jnp.where(pick, 1.0, 0.0).astype(BF)
    return jnp.dot(
        jnp.concatenate(spread, axis=0).astype(BF), pick, preferred_element_type=F32
    )


def unseat(tile, y_hi):
    tile = jnp.where(y_hi == 0, tile, pltpu.roll(tile, 96, 1))
    lane = lax.broadcasted_iota(jnp.int32, (16, ROWS), 1)
    row = lax.broadcasted_iota(jnp.int32, (16, ROWS), 0)
    sums = jnp.zeros((16, ROWS), F32)
    for q in range(4):
        part = tile[:, 16 + q : 17 + q] + tile[:, 20 + q : 21 + q]
        sums = sums + jnp.where((lane >> 2 == row) & (lane & 3 == q), part, 0.0)
    tall = jnp.concatenate([tile, jnp.zeros((112, 128), F32)], axis=0).T
    tile = jnp.where(seated_lanes(0), pltpu.roll(tall[64:80], 16, 1), tile)
    tile = jnp.where(y_hi == 0, tile, pltpu.roll(tile, 32, 1))
    return jnp.sum(sums, axis=0, keepdims=True), tile


def gram_kernel(
    mine, other, base_mean, weight_row, value_row,
    out, transform, gathered, centred, scaled, part,
):
    core = lax.axis_index("core")
    crossed = jnp.where(spot()[1] * COLS < EDGE, GROUP // 2, 0)
    for k in range(GROUP):
        for block, side in ((mine, core), (other, 1 - core)):
            at = pl.ds(pl.multiple_of(k * 128 + side * ROWS, ROWS), ROWS)
            transform[at] = block[k, :, COLS:]
            home = lax.rem(k + crossed, GROUP) * 128 + side * ROWS
            gathered[pl.ds(pl.multiple_of(home, ROWS), ROWS)] = block[k, :, 0:COLS]

    own = [pl.ds(pl.multiple_of(k * 128 + core * ROWS, ROWS), ROWS) for k in range(GROUP)]
    for k in range(COLS // CH):
        c = slice(k * CH, k * CH + CH)
        mean = jnp.dot(transform[...], gathered[:, c], preferred_element_type=F32)
        mean = mean + base_mean[:, c]
        predicted = mean + 0.25 * mean * mean
        average = jnp.sum(predicted, axis=0, keepdims=True) * (1.0 / M)
        difference = predicted - average
        centred[k] = difference
        weight = weight_row[:, c]
        scaled[:, c] = (difference * jnp.sqrt(weight * (1.0 / (M - 1)))).astype(BF)
        slope = (value_row[:, c] - weight * average) * (1.0 / math.sqrt(M - 1))
        for j in range(GROUP):
            product = centred[k, own[j]] * slope
            product = product[:, :128] + product[:, 128:]
            if k == 0:
                part[j * ROWS : j * ROWS + ROWS] = product
            else:
                part[j * ROWS : j * ROWS + ROWS] += product
    rows = jnp.concatenate([scaled[own[j]] for j in range(GROUP)], axis=0)
    slopes = jnp.sum(part[...].T, axis=0, keepdims=True)
    left_half = lax.broadcasted_iota(jnp.int32, (16, 128), 1) < ROWS
    seats = seated(slopes)
    gram = lax.dot_general(scaled[...], rows, NT, preferred_element_type=F32)
    for j in range(GROUP):
        lanes = slice(j // 2 * 128, j // 2 * 128 + 128)
        seat = seats[j * 16 : j * 16 + 16]
        for y_hi in range(2):
            target = out.at[y_hi * GROUP + j]
            for z in range(16):
                at = z * 64 + y_hi * 32
                top = gram[at : at + 16, lanes]
                bottom = gram[at + 16 : at + 32, lanes]
                if j % 2 == 0:
                    packed = jnp.where(left_half, top, pltpu.roll(bottom, ROWS, 1))
                else:
                    packed = jnp.where(left_half, pltpu.roll(top, ROWS, 1), bottom)
                if z // 2 == j:
                    taken = seated_lanes(y_hi) & (core == z % 2)
                    packed = jnp.where(taken, pltpu.roll(seat, 32, 1) if y_hi else seat, packed)
                target[z * 16 : z * 16 + 16] = packed.astype(BF)


def middle_kernel(parts, out, total):
    total[...] = jnp.sum(parts[...].astype(F32), axis=0)
    block = spot()[2] // ROWS
    at = pl.ds(pl.multiple_of(block * 16, 16), 16)
    slopes, tile = unseat(total[at], lax.axis_index("y_hi"))
    total[at] = tile
    tail = two_part_rows(slopes, 16)
    for z in range(16):
        out[z, 0:16] = total[z * 16 : z * 16 + 16].astype(BF)
        out[z, 16:32] = tail


def last_kernel(parts, weights, hessian, gradient):
    _, _, row0, column0 = spot()
    total = jnp.sum(parts[...].astype(F32), axis=0)
    row = lax.broadcasted_iota(jnp.int32, (16, ROWS), 1) + row0
    column = lax.broadcasted_iota(jnp.int32, (16, ROWS), 0) + column0
    for half in range(2):
        block = total[0:16, half * ROWS : half * ROWS + ROWS]
        same = row == column + half * 16
        hessian[half * 16 : half * 16 + 16] = block + jnp.where(same, 1.0, 0.0)
    gradient[...] = weights[...] - (total[16:17, 0:ROWS] + total[16:17, ROWS:])


def on_device(base_state, anomalies, transform, weights, observed, obs_scale, obs_rows, offsets):
    row = lambda v: v.reshape(1, S)
    base = row(base_state)
    obs = (row(observed), row(obs_scale), row(obs_rows))

    edge, first = call(
        edge_kernel,
        (shape(PITCH, EDGE), shape(ROWS, EDGE)),
        [hbm()] * 5,
        scratch=[
            pltpu.VMEM((1, EDGE), F32),
            pltpu.VMEM((1, S), F32),
            pltpu.VMEM((1, S), F32),
            pltpu.VMEM((1, S), jnp.int32),
            pltpu.SemaphoreType.DMA((6,)),
        ],
        flops=4 * 10**9,
        nbytes=MIB,
        limit=FULL,
    )(anomalies, base, *obs)
    onward = [(d, (d + 2) % 64 ^ 1) for d in range(64)]
    edge = lax.ppermute(edge, ("z", "y_hi", "y_lo"), onward)
    first = lax.ppermute(first, "y_lo", [(0, 1), (1, 0)])

    outgoing, band, border, means = call(
        inner_kernel,
        (
            shape(GROUP, ROWS, COLS + M),
            shape(TILES * CH, CH),
            shape(OUTER * 16, CH),
            shape32(1, S),
        ),
        [smem()] + [vmem()] * 2 + [hbm()],
        scratch=[
            pltpu.VMEM((S // CH * PITCH, CH), BF),
            pltpu.SemaphoreType.DMA((GROUP,)),
        ],
        flops=2 * INNER * PITCH * TILES * CH * CH,
        nbytes=4 * MIB,
    )(offsets, anomalies, base, transform)
    anywhere = pl.BlockSpec(memory_space=pl.ANY)
    outgoing, base_mean = call(
        outer_kernel,
        (shape(GROUP, ROWS, COLS + M), shape32(1, COLS)),
        [vmem()] * 5 + [anywhere],
        scratch=[
            pltpu.VMEM((2 * OUTER * PITCH, CH), BF),
            pltpu.VMEM((1, S), F32),
            pltpu.VMEM((2, ROWS, COLS), BF),
            pltpu.SemaphoreType.DMA((2,)),
        ],
        flops=2 * OUTER * PITCH * TILES * CH * CH,
        nbytes=MIB,
        alias={5: 0},
        out_specs=(anywhere, vmem()),
    )(edge, first, band, border, means, outgoing)

    mine = lax.all_to_all(outgoing, ("y_lo", "x"), 0, 0)
    other = lax.ppermute(mine, "core", [(0, 1), (1, 0)])

    weight_row, value_row = call(
        weight_kernel,
        (shape32(1, COLS), shape32(1, COLS)),
        [vmem()] * 4,
        flops=2 * 48 * S * 128,
        nbytes=MIB,
    )(*obs, edge)

    parts = call(
        gram_kernel,
        shape(2 * GROUP, 256, 128),
        [vmem()] * 5,
        scratch=[
            pltpu.VMEM((M, M), BF),
            pltpu.VMEM((M, COLS), BF),
            pltpu.VMEM((COLS // CH, M, CH), F32),
            pltpu.VMEM((M, COLS), BF),
            pltpu.VMEM((GROUP * ROWS, 128), F32),
        ],
        flops=2 * M * M * 768,
        nbytes=4 * MIB,
        limit=32,
    )(mine, other, base_mean, weight_row, value_row)
    parts = lax.all_to_all(parts, ("y_hi", "y_lo", "x"), 0, 0)
    sums = call(
        middle_kernel,
        shape(16, 32, 128),
        [vmem()],
        scratch=[pltpu.VMEM((256, 128), F32)],
        nbytes=MIB,
    )(parts)
    sums = lax.all_to_all(sums, "z", 0, 0)
    hessian, gradient = call(
        last_kernel, (shape32(32, ROWS), shape32(1, ROWS)), [vmem()] * 2, nbytes=MIB // 4
    )(sums, weights.reshape(1, ROWS))
    return hessian.T, gradient.reshape(ROWS)


def solution(mesh):
    fine = Mesh(mesh.devices.reshape(16, 2, 2, 4, 2), ("z", "y_hi", "y_lo", "x", "core"))
    state = ("z", "y_hi")
    member = ("y_lo", "x", "core")
    placed = (
        P(state),
        P(member, state),
        P(member, None),
        P(member),
        P(state),
        P(state),
        P(state),
        P(),
    )
    return jax.shard_map(
        on_device,
        mesh=fine,
        in_specs=placed,
        out_specs=(P(member, state), P(member)),
        check_vma=False,
    )
```

```python
import math

import jax
import jax.numpy as jnp
from jax import lax
from jax.experimental import pallas as pl
from jax.experimental.pallas import tpu as pltpu
from jax.sharding import Mesh, PartitionSpec as P

M = 1024
S = 4096
REACH = 512
TAPS = 8
ROWS = 64
GROUP = 8
COLS = S // GROUP
CH = 256
PITCH = 80
EDGE = 2 * REACH
TILES = 2 * REACH // CH + 1
OUTER = EDGE // CH
INNER = S // CH - OUTER
BF = jnp.bfloat16
F32 = jnp.float32
NT = (((1,), (1,)), ((), ()))
MIB = 2**20
FULL = 63


def call(
    kernel, out_shape, in_specs, scratch=(), flops=0, nbytes=0, limit=16, alias=None, out_specs=None
):
    return pl.pallas_call(
        kernel,
        out_shape=out_shape,
        in_specs=in_specs,
        out_specs=out_specs
        or jax.tree.map(lambda _: pl.BlockSpec(memory_space=pltpu.VMEM), out_shape),
        scratch_shapes=list(scratch),
        compiler_params=pltpu.CompilerParams(vmem_limit_bytes=limit * MIB),
        input_output_aliases=alias or {},
        cost_estimate=pl.CostEstimate(flops=flops, bytes_accessed=nbytes, transcendentals=0),
    )


def spot():
    state = lax.axis_index("z") * 2 + lax.axis_index("y_hi")
    column = lax.axis_index("y_lo") * 4 + lax.axis_index("x")
    return state, column, (column * 2 + lax.axis_index("core")) * ROWS, state * 32


def vmem():
    return pl.BlockSpec(memory_space=pltpu.VMEM)


def smem():
    return pl.BlockSpec(memory_space=pltpu.SMEM)


def hbm():
    return pl.BlockSpec(memory_space=pltpu.HBM)


def shape(*dims):
    return jax.ShapeDtypeStruct(dims, BF)


def shape32(*dims):
    return jax.ShapeDtypeStruct(dims, F32)


def three_parts(value):
    high = value.astype(BF)
    rest = value - high.astype(F32)
    middle = rest.astype(BF)
    low = (rest - middle.astype(F32)).astype(BF)
    return high, middle, low


def base_rows(base):
    high, middle, low = three_parts(base)
    zeros = jnp.zeros((13, base.shape[1]), BF)
    return jnp.concatenate([high, middle, low, zeros], axis=0)


def sums_at_rows(first_line, observed, obs_scale, at):
    square = obs_scale * obs_scale
    high = at >> 7
    low = at & 127
    lanes = lax.broadcasted_iota(jnp.int32, (128, S), 0) == low
    lanes = jnp.where(lanes, 1.0, 0.0).astype(BF)
    line = lax.broadcasted_iota(jnp.int32, (8, S), 0)
    term = jnp.where(line < 4, square, square * observed)
    term = jnp.where((line & 3) + first_line == high, term, 0.0)
    left = jnp.concatenate([part.astype(F32) for part in three_parts(term)], axis=0).astype(BF)
    sums = lax.dot_general(left, lanes, NT, preferred_element_type=F32)
    sums = sums[0:8] + sums[8:16] + sums[16:24]
    rows = [jnp.concatenate([sums[k : k + 1] for k in range(at, at + 4)], axis=1) for at in (0, 4)]
    return rows


def edge_kernel(
    anomalies, base, observed, obs_scale, obs_rows, edge, first,
    base_edge, observed_all, scale_all, rows_all, sems,
):
    border = pl.ds(S - EDGE, EDGE)
    copies = [
        pltpu.make_async_copy(obs_rows, rows_all, sems.at[0]),
        pltpu.make_async_copy(obs_scale, scale_all, sems.at[1]),
        pltpu.make_async_copy(observed, observed_all, sems.at[2]),
        pltpu.make_async_copy(base.at[:, border], base_edge, sems.at[3]),
        pltpu.make_async_copy(anomalies.at[:, border], edge.at[pl.ds(0, ROWS)], sems.at[4]),
        pltpu.make_async_copy(anomalies.at[:, pl.ds(0, EDGE)], first, sems.at[5]),
    ]
    for copy in copies:
        copy.start()
    for copy in copies[:4]:
        copy.wait()
    weight, value = sums_at_rows(
        S // 128 - 4, observed_all[...], scale_all[...], rows_all[...] - spot()[0] * S
    )
    empty = jnp.zeros((1, EDGE - REACH), F32)
    extra = list(three_parts(base_edge[...]))
    for row in (weight, value):
        extra += three_parts(jnp.concatenate([empty, row], axis=1))
    extra.append(jnp.zeros((7, EDGE), BF))
    edge[ROWS:] = jnp.concatenate(extra, axis=0)
    copies[4].wait()
    copies[5].wait()


def banded(rows, band, first, count):
    total = jnp.zeros((count * PITCH, CH), F32)
    for k in range(TILES):
        at = (first + k) * PITCH
        total = total + jnp.dot(
            rows[at : at + count * PITCH],
            band[k * CH : k * CH + CH],
            preferred_element_type=F32,
        )
    return total


def put_chunk(total, k, chunk, out, means):
    at = k * PITCH
    out[chunk // 2, :, chunk % 2 * CH : chunk % 2 * CH + CH] = total[at : at + ROWS].astype(BF)
    at = at + ROWS
    means[:, chunk * CH : chunk * CH + CH] = (
        total[at : at + 1] + total[at + 1 : at + 2] + total[at + 2 : at + 3]
    )


def inner_kernel(offsets, anomalies, base, transform, out, band, border, means, rows, sems):
    copies = [
        pltpu.make_async_copy(transform, out.at[k, :, pl.ds(COLS, M)], sems.at[k])
        for k in range(GROUP)
    ]
    for copy in copies:
        copy.start()
    for k in range(S // CH):
        c = slice(k * CH, k * CH + CH)
        at = k * PITCH
        rows[at : at + ROWS] = anomalies[:, c]
        rows[at + ROWS : at + PITCH] = base_rows(base[:, c])
    for k in range(TILES):
        shift = (
            lax.broadcasted_iota(jnp.int32, (CH, CH), 0)
            - lax.broadcasted_iota(jnp.int32, (CH, CH), 1)
            + (k * CH - REACH)
        )
        count = jnp.zeros((CH, CH), F32)
        for tap in range(TAPS):
            count = count + jnp.where(shift == offsets[tap], 1.0 / TAPS, 0.0)
        band[k * CH : k * CH + CH] = count.astype(BF)
    total = banded(rows, band, 0, INNER)
    means[...] = jnp.zeros_like(means)
    for k in range(INNER):
        put_chunk(total, k, k + OUTER, out, means)
    for k in range(OUTER):
        border[k * 16 : k * 16 + 16] = rows[k * PITCH + ROWS : (k + 1) * PITCH]
    for copy in copies:
        copy.wait()


def outer_kernel(
    edge, first, band, border, means_in, out_in, out, base_mean, rows, means, chunks, sems
):
    state, column, _, _ = spot()
    whole = state > 0
    means[...] = means_in[...]
    for k in range(OUTER):
        at = k * PITCH
        rows[at : at + PITCH] = edge[:, k * CH : k * CH + CH]
        at = at + OUTER * PITCH
        rows[at : at + ROWS] = first[:, k * CH : k * CH + CH]
        rows[at + ROWS : at + PITCH] = border[k * 16 : k * 16 + 16]
    seen = jnp.where(whole, 1.0, 0.0).astype(BF)
    before = rows[2 * PITCH : 4 * PITCH]
    after = rows[4 * PITCH : 6 * PITCH]
    rows[4 * PITCH : 6 * PITCH] = after * seen
    total = banded(rows, band, 0, 2)
    for k in range(2):
        put_chunk(total, k, k, chunks, means)
    rows[4 * PITCH : 6 * PITCH] = after
    rows[2 * PITCH : 4 * PITCH] = before * seen
    total = banded(rows, band, 2, 2)
    for k in range(2):
        put_chunk(total, k, k + 2, chunks, means)
    copies = [
        pltpu.make_async_copy(chunks.at[k], out.at[k, :, pl.ds(0, COLS)], sems.at[k])
        for k in range(2)
    ]
    for copy in copies:
        copy.start()
    for copy in copies:
        copy.wait()
    base_mean[...] = means[:, pl.ds(pl.multiple_of(column * COLS, COLS), COLS)]


def weight_kernel(observed, obs_scale, obs_rows, edge, weight_row, value_row):
    state, column, _, _ = spot()
    weight, value = sums_at_rows(
        (column - 1) * 4, observed[...], obs_scale[...], obs_rows[...] - state * S
    )
    half = pl.ds(EDGE - REACH, REACH)
    row = lambda k: edge[ROWS : ROWS + 16, half][k : k + 1].astype(F32)
    mine = column > 0
    for own, target, at in ((weight, weight_row, 3), (value, value_row, 6)):
        sent = row(at) + row(at + 1) + row(at + 2)
        target[...] = jnp.where(mine, own, sent)


def two_part_rows(value, count):
    high = value.astype(BF).astype(F32)
    low = value - high
    row = jnp.concatenate([high, low], axis=1)
    return jnp.concatenate([row, jnp.zeros((count - 1, 128), F32)], axis=0).astype(BF)


def seated_lanes(y_hi):
    lane = lax.broadcasted_iota(jnp.int32, (16, 128), 1)
    return (lane >= 16 + 32 * y_hi) & (lane < 24 + 32 * y_hi)


def seated(slopes):
    lane = lax.broadcasted_iota(jnp.int32, (16, 128), 1)
    mine = ((lane & (ROWS - 1)) >> 2) == lax.broadcasted_iota(jnp.int32, (16, 128), 0)
    high = slopes.astype(BF).astype(F32)
    low = slopes - high
    spread = []
    for j in range(GROUP):
        c = slice(j * ROWS, j * ROWS + ROWS)
        row = jnp.concatenate([high[:, c], low[:, c]], axis=1)
        spread.append(jnp.where(mine, row, 0.0))
    source = lax.broadcasted_iota(jnp.int32, (128, 128), 0)
    target = 16 + (source & 3) + jnp.where(source >= ROWS, 4, 0)
    pick = lax.broadcasted_iota(jnp.int32, (128, 128), 1) == target
    pick = jnp.where(pick, 1.0, 0.0).astype(BF)
    return jnp.dot(
        jnp.concatenate(spread, axis=0).astype(BF), pick, preferred_element_type=F32
    )


def unseat(tile, y_hi):
    tile = jnp.where(y_hi == 0, tile, pltpu.roll(tile, 96, 1))
    lane = lax.broadcasted_iota(jnp.int32, (16, ROWS), 1)
    row = lax.broadcasted_iota(jnp.int32, (16, ROWS), 0)
    sums = jnp.zeros((16, ROWS), F32)
    for q in range(4):
        part = tile[:, 16 + q : 17 + q] + tile[:, 20 + q : 21 + q]
        sums = sums + jnp.where((lane >> 2 == row) & (lane & 3 == q), part, 0.0)
    tall = jnp.concatenate([tile, jnp.zeros((112, 128), F32)], axis=0).T
    tile = jnp.where(seated_lanes(0), pltpu.roll(tall[64:80], 16, 1), tile)
    tile = jnp.where(y_hi == 0, tile, pltpu.roll(tile, 32, 1))
    return jnp.sum(sums, axis=0, keepdims=True), tile


def gram_kernel(
    mine, other, base_mean, weight_row, value_row,
    out, gathered, scaled, part,
):
    core = lax.axis_index("core")
    crossed = jnp.where(spot()[1] * COLS < EDGE, GROUP // 2, 0)
    for k in range(GROUP):
        for block, side in ((mine, core), (other, 1 - core)):
            home = lax.rem(k + crossed, GROUP) * 128 + side * ROWS
            gathered[pl.ds(pl.multiple_of(home, ROWS), ROWS)] = block[k, :, 0:COLS]

    half = GROUP * ROWS
    for k in range(COLS // CH):
        c = slice(k * CH, k * CH + CH)
        predicted = []
        for block in (mine, other):
            mean = jnp.dot(
                block[:, :, COLS:].reshape(half, M), gathered[:, c], preferred_element_type=F32
            )
            mean = mean + base_mean[:, c]
            predicted.append(mean + 0.25 * mean * mean)
        average = jnp.sum(predicted[0] + predicted[1], axis=0, keepdims=True) * (1.0 / M)
        weight = weight_row[:, c]
        root = jnp.sqrt(weight * (1.0 / (M - 1)))
        slope = (value_row[:, c] - weight * average) * (1.0 / math.sqrt(M - 1))
        for n in range(2):
            difference = predicted[n] - average
            scaled[n * half : n * half + half, c] = (difference * root).astype(BF)
            if n == 0:
                product = difference * slope
                product = product[:, :128] + product[:, 128:]
                if k == 0:
                    part[...] = product
                else:
                    part[...] += product
    slopes = jnp.sum(part[...].T, axis=0, keepdims=True)
    left_half = lax.broadcasted_iota(jnp.int32, (16, 128), 1) < ROWS
    seats = seated(slopes)
    gram = lax.dot_general(scaled[...], scaled[0:half], NT, preferred_element_type=F32)
    here = [core == n for n in range(2)]
    for j in range(GROUP):
        lanes = slice(j // 2 * 128, j // 2 * 128 + 128)
        seat = seats[j * 16 : j * 16 + 16]
        for y_hi in range(2):
            target = out.at[y_hi * GROUP + j]
            for z in range(16):
                at = z // 2 * ROWS + y_hi * 32
                both = jnp.where(
                    here[z % 2], gram[at : at + 32, lanes], gram[half + at : half + at + 32, lanes]
                )
                top, bottom = both[0:16], both[16:32]
                if j % 2 == 0:
                    packed = jnp.where(left_half, top, pltpu.roll(bottom, ROWS, 1))
                else:
                    packed = jnp.where(left_half, pltpu.roll(top, ROWS, 1), bottom)
                if z // 2 == j:
                    taken = seated_lanes(y_hi) & (core == z % 2)
                    packed = jnp.where(taken, pltpu.roll(seat, 32, 1) if y_hi else seat, packed)
                target[z * 16 : z * 16 + 16] = packed.astype(BF)


def middle_kernel(parts, out, total):
    total[...] = jnp.sum(parts[...].astype(F32), axis=0)
    block = spot()[2] // ROWS
    at = pl.ds(pl.multiple_of(block * 16, 16), 16)
    slopes, tile = unseat(total[at], lax.axis_index("y_hi"))
    total[at] = tile
    tail = two_part_rows(slopes, 16)
    for z in range(16):
        out[z, 0:16] = total[z * 16 : z * 16 + 16].astype(BF)
        out[z, 16:32] = tail


def last_kernel(parts, weights, hessian, gradient):
    _, _, row0, column0 = spot()
    total = jnp.sum(parts[...].astype(F32), axis=0)
    row = lax.broadcasted_iota(jnp.int32, (16, ROWS), 1) + row0
    column = lax.broadcasted_iota(jnp.int32, (16, ROWS), 0) + column0
    for half in range(2):
        block = total[0:16, half * ROWS : half * ROWS + ROWS]
        same = row == column + half * 16
        hessian[half * 16 : half * 16 + 16] = block + jnp.where(same, 1.0, 0.0)
    gradient[...] = weights[...] - (total[16:17, 0:ROWS] + total[16:17, ROWS:])


def on_device(base_state, anomalies, transform, weights, observed, obs_scale, obs_rows, offsets):
    row = lambda v: v.reshape(1, S)
    base = row(base_state)
    obs = (row(observed), row(obs_scale), row(obs_rows))

    edge, first = call(
        edge_kernel,
        (shape(PITCH, EDGE), shape(ROWS, EDGE)),
        [hbm()] * 5,
        scratch=[
            pltpu.VMEM((1, EDGE), F32),
            pltpu.VMEM((1, S), F32),
            pltpu.VMEM((1, S), F32),
            pltpu.VMEM((1, S), jnp.int32),
            pltpu.SemaphoreType.DMA((6,)),
        ],
        flops=4 * 10**9,
        nbytes=MIB,
        limit=FULL,
    )(anomalies, base, *obs)
    onward = [(d, (d + 2) % 64 ^ 1) for d in range(64)]
    edge = lax.ppermute(edge, ("z", "y_hi", "y_lo"), onward)
    first = lax.ppermute(first, "y_lo", [(0, 1), (1, 0)])

    outgoing, band, border, means = call(
        inner_kernel,
        (
            shape(GROUP, ROWS, COLS + M),
            shape(TILES * CH, CH),
            shape(OUTER * 16, CH),
            shape32(1, S),
        ),
        [smem()] + [vmem()] * 2 + [hbm()],
        scratch=[
            pltpu.VMEM((S // CH * PITCH, CH), BF),
            pltpu.SemaphoreType.DMA((GROUP,)),
        ],
        flops=2 * INNER * PITCH * TILES * CH * CH,
        nbytes=4 * MIB,
    )(offsets, anomalies, base, transform)
    anywhere = pl.BlockSpec(memory_space=pl.ANY)
    outgoing, base_mean = call(
        outer_kernel,
        (shape(GROUP, ROWS, COLS + M), shape32(1, COLS)),
        [vmem()] * 5 + [anywhere],
        scratch=[
            pltpu.VMEM((2 * OUTER * PITCH, CH), BF),
            pltpu.VMEM((1, S), F32),
            pltpu.VMEM((2, ROWS, COLS), BF),
            pltpu.SemaphoreType.DMA((2,)),
        ],
        flops=2 * OUTER * PITCH * TILES * CH * CH,
        nbytes=MIB,
        alias={5: 0},
        out_specs=(anywhere, vmem()),
    )(edge, first, band, border, means, outgoing)

    mine = lax.all_to_all(outgoing, ("y_lo", "x"), 0, 0)
    other = lax.ppermute(mine, "core", [(0, 1), (1, 0)])

    weight_row, value_row = call(
        weight_kernel,
        (shape32(1, COLS), shape32(1, COLS)),
        [vmem()] * 4,
        flops=2 * 48 * S * 128,
        nbytes=MIB,
    )(*obs, edge)

    parts = call(
        gram_kernel,
        shape(2 * GROUP, 256, 128),
        [vmem()] * 5,
        scratch=[
            pltpu.VMEM((M, COLS), BF),
            pltpu.VMEM((M, COLS), BF),
            pltpu.VMEM((GROUP * ROWS, 128), F32),
        ],
        flops=2 * M * M * 768,
        nbytes=4 * MIB,
        limit=32,
    )(mine, other, base_mean, weight_row, value_row)
    parts = lax.all_to_all(parts, ("y_hi", "y_lo", "x"), 0, 0)
    sums = call(
        middle_kernel,
        shape(16, 32, 128),
        [vmem()],
        scratch=[pltpu.VMEM((256, 128), F32)],
        nbytes=MIB,
    )(parts)
    sums = lax.all_to_all(sums, "z", 0, 0)
    hessian, gradient = call(
        last_kernel, (shape32(32, ROWS), shape32(1, ROWS)), [vmem()] * 2, nbytes=MIB // 4
    )(sums, weights.reshape(1, ROWS))
    return hessian.T, gradient.reshape(ROWS)


def solution(mesh):
    fine = Mesh(mesh.devices.reshape(16, 2, 2, 4, 2), ("z", "y_hi", "y_lo", "x", "core"))
    state = ("z", "y_hi")
    member = ("y_lo", "x", "core")
    placed = (
        P(state),
        P(member, state),
        P(member, None),
        P(member),
        P(state),
        P(state),
        P(state),
        P(),
    )
    return jax.shard_map(
        on_device,
        mesh=fine,
        in_specs=placed,
        out_specs=(P(member, state), P(member)),
        check_vma=False,
    )
```

```python
import math

import jax
import jax.numpy as jnp
from jax import lax
from jax.experimental import pallas as pl
from jax.experimental.pallas import tpu as pltpu
from jax.sharding import Mesh, PartitionSpec as P

M = 1024
S = 4096
REACH = 512
TAPS = 8
ROWS = 64
GROUP = 8
COLS = S // GROUP
CH = 256
PITCH = 80
EDGE = 2 * REACH
TILES = 2 * REACH // CH + 1
OUTER = EDGE // CH
INNER = S // CH - OUTER
BF = jnp.bfloat16
F32 = jnp.float32
NT = (((1,), (1,)), ((), ()))
MIB = 2**20
FULL = 63


def call(
    kernel, out_shape, in_specs, scratch=(), flops=0, nbytes=0, limit=16, alias=None, out_specs=None
):
    return pl.pallas_call(
        kernel,
        out_shape=out_shape,
        in_specs=in_specs,
        out_specs=out_specs
        or jax.tree.map(lambda _: pl.BlockSpec(memory_space=pltpu.VMEM), out_shape),
        scratch_shapes=list(scratch),
        compiler_params=pltpu.CompilerParams(vmem_limit_bytes=limit * MIB),
        input_output_aliases=alias or {},
        cost_estimate=pl.CostEstimate(flops=flops, bytes_accessed=nbytes, transcendentals=0),
    )


def spot():
    state = lax.axis_index("z") * 2 + lax.axis_index("y_hi")
    column = lax.axis_index("y_lo") * 4 + lax.axis_index("x")
    return state, column, (column * 2 + lax.axis_index("core")) * ROWS, state * 32


def vmem():
    return pl.BlockSpec(memory_space=pltpu.VMEM)


def smem():
    return pl.BlockSpec(memory_space=pltpu.SMEM)


def hbm():
    return pl.BlockSpec(memory_space=pltpu.HBM)


def shape(*dims):
    return jax.ShapeDtypeStruct(dims, BF)


def shape32(*dims):
    return jax.ShapeDtypeStruct(dims, F32)


def three_parts(value):
    high = value.astype(BF)
    rest = value - high.astype(F32)
    middle = rest.astype(BF)
    low = (rest - middle.astype(F32)).astype(BF)
    return high, middle, low


def base_rows(base):
    high, middle, low = three_parts(base)
    zeros = jnp.zeros((13, base.shape[1]), BF)
    return jnp.concatenate([high, middle, low, zeros], axis=0)


def sums_at_rows(first_line, observed, obs_scale, at):
    square = obs_scale * obs_scale
    high = at >> 7
    low = at & 127
    lanes = lax.broadcasted_iota(jnp.int32, (128, S), 0) == low
    lanes = jnp.where(lanes, 1.0, 0.0).astype(BF)
    line = lax.broadcasted_iota(jnp.int32, (8, S), 0)
    term = jnp.where(line < 4, square, square * observed)
    term = jnp.where((line & 3) + first_line == high, term, 0.0)
    left = jnp.concatenate([part.astype(F32) for part in three_parts(term)], axis=0).astype(BF)
    sums = lax.dot_general(left, lanes, NT, preferred_element_type=F32)
    sums = sums[0:8] + sums[8:16] + sums[16:24]
    rows = [jnp.concatenate([sums[k : k + 1] for k in range(at, at + 4)], axis=1) for at in (0, 4)]
    return rows


def edge_kernel(
    anomalies, base, observed, obs_scale, obs_rows, edge, first,
    base_edge, observed_all, scale_all, rows_all, sems,
):
    border = pl.ds(S - EDGE, EDGE)
    copies = [
        pltpu.make_async_copy(obs_rows, rows_all, sems.at[0]),
        pltpu.make_async_copy(obs_scale, scale_all, sems.at[1]),
        pltpu.make_async_copy(observed, observed_all, sems.at[2]),
        pltpu.make_async_copy(base.at[:, border], base_edge, sems.at[3]),
        pltpu.make_async_copy(anomalies.at[:, border], edge.at[pl.ds(0, ROWS)], sems.at[4]),
        pltpu.make_async_copy(anomalies.at[:, pl.ds(0, EDGE)], first, sems.at[5]),
    ]
    for copy in copies:
        copy.start()
    for copy in copies[:4]:
        copy.wait()
    weight, value = sums_at_rows(
        S // 128 - 4, observed_all[...], scale_all[...], rows_all[...] - spot()[0] * S
    )
    empty = jnp.zeros((1, EDGE - REACH), F32)
    extra = list(three_parts(base_edge[...]))
    for row in (weight, value):
        extra += three_parts(jnp.concatenate([empty, row], axis=1))
    extra.append(jnp.zeros((7, EDGE), BF))
    edge[ROWS:] = jnp.concatenate(extra, axis=0)
    copies[4].wait()
    copies[5].wait()


def banded(rows, band, first, count):
    total = jnp.zeros((count * PITCH, CH), F32)
    for k in range(TILES):
        at = (first + k) * PITCH
        total = total + jnp.dot(
            rows[at : at + count * PITCH],
            band[k * CH : k * CH + CH],
            preferred_element_type=F32,
        )
    return total


def put_chunk(total, k, chunk, out, means):
    at = k * PITCH
    out[chunk // 2, :, chunk % 2 * CH : chunk % 2 * CH + CH] = total[at : at + ROWS].astype(BF)
    at = at + ROWS
    means[:, chunk * CH : chunk * CH + CH] = (
        total[at : at + 1] + total[at + 1 : at + 2] + total[at + 2 : at + 3]
    )


def inner_kernel(offsets, anomalies, base, transform, out, band, border, means, rows, sems):
    copies = [
        pltpu.make_async_copy(transform, out.at[k, :, pl.ds(COLS, M)], sems.at[k])
        for k in range(GROUP)
    ]
    for copy in copies:
        copy.start()
    for k in range(S // CH):
        c = slice(k * CH, k * CH + CH)
        at = k * PITCH
        rows[at : at + ROWS] = anomalies[:, c]
        rows[at + ROWS : at + PITCH] = base_rows(base[:, c])
    for k in range(TILES):
        shift = (
            lax.broadcasted_iota(jnp.int32, (CH, CH), 0)
            - lax.broadcasted_iota(jnp.int32, (CH, CH), 1)
            + (k * CH - REACH)
        )
        count = jnp.zeros((CH, CH), F32)
        for tap in range(TAPS):
            count = count + jnp.where(shift == offsets[tap], 1.0 / TAPS, 0.0)
        band[k * CH : k * CH + CH] = count.astype(BF)
    total = banded(rows, band, 0, INNER)
    means[...] = jnp.zeros_like(means)
    for k in range(INNER):
        put_chunk(total, k, k + OUTER, out, means)
    for k in range(OUTER):
        border[k * 16 : k * 16 + 16] = rows[k * PITCH + ROWS : (k + 1) * PITCH]
    for copy in copies:
        copy.wait()


def outer_kernel(
    edge, first, band, border, means_in, out_in, out, base_mean, rows, means, chunks, sems
):
    state, column, _, _ = spot()
    whole = state > 0
    means[...] = means_in[...]
    for k in range(OUTER):
        at = k * PITCH
        rows[at : at + PITCH] = edge[:, k * CH : k * CH + CH]
        at = at + OUTER * PITCH
        rows[at : at + ROWS] = first[:, k * CH : k * CH + CH]
        rows[at + ROWS : at + PITCH] = border[k * 16 : k * 16 + 16]
    seen = jnp.where(whole, 1.0, 0.0).astype(BF)
    before = rows[2 * PITCH : 4 * PITCH]
    after = rows[4 * PITCH : 6 * PITCH]
    rows[4 * PITCH : 6 * PITCH] = after * seen
    total = banded(rows, band, 0, 2)
    for k in range(2):
        put_chunk(total, k, k, chunks, means)
    rows[4 * PITCH : 6 * PITCH] = after
    rows[2 * PITCH : 4 * PITCH] = before * seen
    total = banded(rows, band, 2, 2)
    for k in range(2):
        put_chunk(total, k, k + 2, chunks, means)
    copies = [
        pltpu.make_async_copy(chunks.at[k], out.at[k, :, pl.ds(0, COLS)], sems.at[k])
        for k in range(2)
    ]
    for copy in copies:
        copy.start()
    for copy in copies:
        copy.wait()
    base_mean[...] = means[:, pl.ds(pl.multiple_of(column * COLS, COLS), COLS)]


def weight_kernel(observed, obs_scale, obs_rows, edge, weight_row, value_row):
    state, column, _, _ = spot()
    weight, value = sums_at_rows(
        (column - 1) * 4, observed[...], obs_scale[...], obs_rows[...] - state * S
    )
    half = pl.ds(EDGE - REACH, REACH)
    row = lambda k: edge[ROWS : ROWS + 16, half][k : k + 1].astype(F32)
    mine = column > 0
    for own, target, at in ((weight, weight_row, 3), (value, value_row, 6)):
        sent = row(at) + row(at + 1) + row(at + 2)
        target[...] = jnp.where(mine, own, sent)


def two_part_rows(value, count):
    high = value.astype(BF).astype(F32)
    low = value - high
    row = jnp.concatenate([high, low], axis=1)
    return jnp.concatenate([row, jnp.zeros((count - 1, 128), F32)], axis=0).astype(BF)


def seated_lanes(y_hi):
    lane = lax.broadcasted_iota(jnp.int32, (16, 128), 1)
    return (lane >= 16 + 32 * y_hi) & (lane < 24 + 32 * y_hi)


def seated(slopes):
    lane = lax.broadcasted_iota(jnp.int32, (16, 128), 1)
    mine = ((lane & (ROWS - 1)) >> 2) == lax.broadcasted_iota(jnp.int32, (16, 128), 0)
    high = slopes.astype(BF).astype(F32)
    low = slopes - high
    spread = []
    for j in range(GROUP):
        c = slice(j * ROWS, j * ROWS + ROWS)
        row = jnp.concatenate([high[:, c], low[:, c]], axis=1)
        spread.append(jnp.where(mine, row, 0.0))
    source = lax.broadcasted_iota(jnp.int32, (128, 128), 0)
    target = 16 + (source & 3) + jnp.where(source >= ROWS, 4, 0)
    pick = lax.broadcasted_iota(jnp.int32, (128, 128), 1) == target
    pick = jnp.where(pick, 1.0, 0.0).astype(BF)
    return jnp.dot(
        jnp.concatenate(spread, axis=0).astype(BF), pick, preferred_element_type=F32
    )


def first_half(tile, y_hi):
    return jnp.where(y_hi == 0, tile, pltpu.roll(tile, 96, 1))


def read_seats(tile, y_hi):
    tile = first_half(tile, y_hi)
    lane = lax.broadcasted_iota(jnp.int32, (16, ROWS), 1)
    row = lax.broadcasted_iota(jnp.int32, (16, ROWS), 0)
    sums = jnp.zeros((16, ROWS), F32)
    for q in range(4):
        part = tile[:, 16 + q : 17 + q] + tile[:, 20 + q : 21 + q]
        sums = sums + jnp.where((lane >> 2 == row) & (lane & 3 == q), part, 0.0)
    return jnp.sum(sums, axis=0, keepdims=True)


def refill_seats(tile, y_hi):
    tile = first_half(tile, y_hi)
    tall = jnp.concatenate([tile, jnp.zeros((112, 128), F32)], axis=0).T
    tile = jnp.where(seated_lanes(0), pltpu.roll(tall[64:80], 16, 1), tile)
    return jnp.where(y_hi == 0, tile, pltpu.roll(tile, 32, 1))


def gram_kernel(
    mine, other, base_mean, weight_row, value_row,
    out, gathered, scaled, part,
):
    core = lax.axis_index("core")
    crossed = jnp.where(spot()[1] * COLS < EDGE, GROUP // 2, 0)
    for k in range(GROUP):
        for block, side in ((mine, core), (other, 1 - core)):
            home = lax.rem(k + crossed, GROUP) * 128 + side * ROWS
            gathered[pl.ds(pl.multiple_of(home, ROWS), ROWS)] = block[k, :, 0:COLS]

    half = GROUP * ROWS
    for k in range(COLS // CH):
        c = slice(k * CH, k * CH + CH)
        predicted = []
        for block in (mine, other):
            mean = jnp.dot(
                block[:, :, COLS:].reshape(half, M), gathered[:, c], preferred_element_type=F32
            )
            mean = mean + base_mean[:, c]
            predicted.append(mean + 0.25 * mean * mean)
        average = jnp.sum(predicted[0] + predicted[1], axis=0, keepdims=True) * (1.0 / M)
        weight = weight_row[:, c]
        root = jnp.sqrt(weight * (1.0 / (M - 1)))
        slope = (value_row[:, c] - weight * average) * (1.0 / math.sqrt(M - 1))
        for n in range(2):
            difference = predicted[n] - average
            scaled[n * half : n * half + half, c] = (difference * root).astype(BF)
            if n == 0:
                product = difference * slope
                product = product[:, :128] + product[:, 128:]
                if k == 0:
                    part[...] = product
                else:
                    part[...] += product
    slopes = jnp.sum(part[...].T, axis=0, keepdims=True)
    left_half = lax.broadcasted_iota(jnp.int32, (16, 128), 1) < ROWS
    seats = seated(slopes)
    gram = lax.dot_general(scaled[...], scaled[0:half], NT, preferred_element_type=F32)
    here = [core == n for n in range(2)]
    for j in range(GROUP):
        lanes = slice(j // 2 * 128, j // 2 * 128 + 128)
        seat = seats[j * 16 : j * 16 + 16]
        for y_hi in range(2):
            target = out.at[y_hi * GROUP + j]
            for z in range(16):
                at = z // 2 * ROWS + y_hi * 32
                both = jnp.where(
                    here[z % 2], gram[at : at + 32, lanes], gram[half + at : half + at + 32, lanes]
                )
                top, bottom = both[0:16], both[16:32]
                if j % 2 == 0:
                    packed = jnp.where(left_half, top, pltpu.roll(bottom, ROWS, 1))
                else:
                    packed = jnp.where(left_half, pltpu.roll(top, ROWS, 1), bottom)
                if z // 2 == j:
                    taken = seated_lanes(y_hi) & (core == z % 2)
                    packed = jnp.where(taken, pltpu.roll(seat, 32, 1) if y_hi else seat, packed)
                target[z * 16 : z * 16 + 16] = packed.astype(BF)


def middle_kernel(parts, out, total):
    for first in range(0, 256, 64):
        rows = slice(first, first + 64)
        sums = parts[0, rows].astype(F32)
        for k in range(1, 2 * GROUP):
            sums = sums + parts[k, rows].astype(F32)
        total[rows] = sums
        for z in range(first // 16, first // 16 + 4):
            at = z * 16 - first
            out[z, 0:16] = sums[at : at + 16].astype(BF)
    block = spot()[2] // ROWS
    at = pl.ds(pl.multiple_of(block * 16, 16), 16)
    tail = two_part_rows(read_seats(total[at], lax.axis_index("y_hi")), 16)
    for z in range(16):
        out[z, 16:32] = tail


def last_kernel(parts, weights, hessian, gradient, packed):
    _, _, row0, column0 = spot()
    total = parts[0].astype(F32)
    for z in range(1, 16):
        total = total + parts[z].astype(F32)
    packed[...] = total[0:16]

    @pl.when(lax.axis_index("z") == row0 // ROWS)
    def _():
        packed[...] = refill_seats(packed[...], lax.axis_index("y_hi"))

    row = lax.broadcasted_iota(jnp.int32, (16, ROWS), 1) + row0
    column = lax.broadcasted_iota(jnp.int32, (16, ROWS), 0) + column0
    for half in range(2):
        block = packed[:, half * ROWS : half * ROWS + ROWS]
        same = row == column + half * 16
        hessian[half * 16 : half * 16 + 16] = block + jnp.where(same, 1.0, 0.0)
    gradient[...] = weights[...] - (total[16:17, 0:ROWS] + total[16:17, ROWS:])


def on_device(base_state, anomalies, transform, weights, observed, obs_scale, obs_rows, offsets):
    row = lambda v: v.reshape(1, S)
    base = row(base_state)
    obs = (row(observed), row(obs_scale), row(obs_rows))

    edge, first = call(
        edge_kernel,
        (shape(PITCH, EDGE), shape(ROWS, EDGE)),
        [hbm()] * 5,
        scratch=[
            pltpu.VMEM((1, EDGE), F32),
            pltpu.VMEM((1, S), F32),
            pltpu.VMEM((1, S), F32),
            pltpu.VMEM((1, S), jnp.int32),
            pltpu.SemaphoreType.DMA((6,)),
        ],
        flops=4 * 10**9,
        nbytes=MIB,
        limit=FULL,
    )(anomalies, base, *obs)
    onward = [(d, (d + 2) % 64 ^ 1) for d in range(64)]
    edge = lax.ppermute(edge, ("z", "y_hi", "y_lo"), onward)
    first = lax.ppermute(first, "y_lo", [(0, 1), (1, 0)])

    outgoing, band, border, means = call(
        inner_kernel,
        (
            shape(GROUP, ROWS, COLS + M),
            shape(TILES * CH, CH),
            shape(OUTER * 16, CH),
            shape32(1, S),
        ),
        [smem()] + [vmem()] * 2 + [hbm()],
        scratch=[
            pltpu.VMEM((S // CH * PITCH, CH), BF),
            pltpu.SemaphoreType.DMA((GROUP,)),
        ],
        flops=2 * INNER * PITCH * TILES * CH * CH,
        nbytes=4 * MIB,
    )(offsets, anomalies, base, transform)
    anywhere = pl.BlockSpec(memory_space=pl.ANY)
    outgoing, base_mean = call(
        outer_kernel,
        (shape(GROUP, ROWS, COLS + M), shape32(1, COLS)),
        [vmem()] * 5 + [anywhere],
        scratch=[
            pltpu.VMEM((2 * OUTER * PITCH, CH), BF),
            pltpu.VMEM((1, S), F32),
            pltpu.VMEM((2, ROWS, COLS), BF),
            pltpu.SemaphoreType.DMA((2,)),
        ],
        flops=2 * OUTER * PITCH * TILES * CH * CH,
        nbytes=MIB,
        alias={5: 0},
        out_specs=(anywhere, vmem()),
    )(edge, first, band, border, means, outgoing)

    mine = lax.all_to_all(outgoing, ("y_lo", "x"), 0, 0)
    other = lax.ppermute(mine, "core", [(0, 1), (1, 0)])

    weight_row, value_row = call(
        weight_kernel,
        (shape32(1, COLS), shape32(1, COLS)),
        [vmem()] * 4,
        flops=2 * 48 * S * 128,
        nbytes=MIB,
    )(*obs, edge)

    parts = call(
        gram_kernel,
        shape(2 * GROUP, 256, 128),
        [vmem()] * 5,
        scratch=[
            pltpu.VMEM((M, COLS), BF),
            pltpu.VMEM((M, COLS), BF),
            pltpu.VMEM((GROUP * ROWS, 128), F32),
        ],
        flops=2 * M * M * 768,
        nbytes=4 * MIB,
        limit=32,
    )(mine, other, base_mean, weight_row, value_row)
    parts = lax.all_to_all(parts, ("y_hi", "y_lo", "x"), 0, 0)
    sums = call(
        middle_kernel,
        shape(16, 32, 128),
        [vmem()],
        scratch=[pltpu.VMEM((256, 128), F32)],
        nbytes=MIB,
    )(parts)
    sums = lax.all_to_all(sums, "z", 0, 0)
    hessian, gradient = call(
        last_kernel, (shape32(32, ROWS), shape32(1, ROWS)), [vmem()] * 2, nbytes=MIB // 4,
        scratch=[pltpu.VMEM((16, 128), F32)],
    )(sums, weights.reshape(1, ROWS))
    return hessian.T, gradient.reshape(ROWS)


def solution(mesh):
    fine = Mesh(mesh.devices.reshape(16, 2, 2, 4, 2), ("z", "y_hi", "y_lo", "x", "core"))
    state = ("z", "y_hi")
    member = ("y_lo", "x", "core")
    placed = (
        P(state),
        P(member, state),
        P(member, None),
        P(member),
        P(state),
        P(state),
        P(state),
        P(),
    )
    return jax.shard_map(
        on_device,
        mesh=fine,
        in_specs=placed,
        out_specs=(P(member, state), P(member)),
        check_vma=False,
    )
```

```python
import math

import jax
import jax.numpy as jnp
from jax import lax
from jax.experimental import pallas as pl
from jax.experimental.pallas import tpu as pltpu
from jax.sharding import Mesh, PartitionSpec as P

M = 1024
S = 4096
REACH = 512
TAPS = 8
ROWS = 64
GROUP = 8
COLS = S // GROUP
CH = 256
PITCH = 80
EDGE = 2 * REACH
TILES = 2 * REACH // CH + 1
OUTER = EDGE // CH
INNER = S // CH - OUTER
BF = jnp.bfloat16
F32 = jnp.float32
NT = (((1,), (1,)), ((), ()))
MIB = 2**20
FULL = 63


def call(
    kernel, out_shape, in_specs, scratch=(), flops=0, nbytes=0, limit=16, alias=None, out_specs=None
):
    return pl.pallas_call(
        kernel,
        out_shape=out_shape,
        in_specs=in_specs,
        out_specs=out_specs
        or jax.tree.map(lambda _: pl.BlockSpec(memory_space=pltpu.VMEM), out_shape),
        scratch_shapes=list(scratch),
        compiler_params=pltpu.CompilerParams(vmem_limit_bytes=limit * MIB),
        input_output_aliases=alias or {},
        cost_estimate=pl.CostEstimate(flops=flops, bytes_accessed=nbytes, transcendentals=0),
    )


def spot():
    state = lax.axis_index("z") * 2 + lax.axis_index("y_hi")
    column = lax.axis_index("y_lo") * 4 + lax.axis_index("x")
    return state, column, (column * 2 + lax.axis_index("core")) * ROWS, state * 32


def vmem():
    return pl.BlockSpec(memory_space=pltpu.VMEM)


def smem():
    return pl.BlockSpec(memory_space=pltpu.SMEM)


def hbm():
    return pl.BlockSpec(memory_space=pltpu.HBM)


def shape(*dims):
    return jax.ShapeDtypeStruct(dims, BF)


def shape32(*dims):
    return jax.ShapeDtypeStruct(dims, F32)


def three_parts(value):
    high = value.astype(BF)
    rest = value - high.astype(F32)
    middle = rest.astype(BF)
    low = (rest - middle.astype(F32)).astype(BF)
    return high, middle, low


def base_rows(base):
    high, middle, low = three_parts(base)
    zeros = jnp.zeros((13, base.shape[1]), BF)
    return jnp.concatenate([high, middle, low, zeros], axis=0)


def sums_at_rows(first_line, observed, obs_scale, at):
    square = obs_scale * obs_scale
    high = at >> 7
    low = at & 127
    lanes = lax.broadcasted_iota(jnp.int32, (128, S), 0) == low
    lanes = jnp.where(lanes, 1.0, 0.0).astype(BF)
    line = lax.broadcasted_iota(jnp.int32, (8, S), 0)
    term = jnp.where(line < 4, square, square * observed)
    term = jnp.where((line & 3) + first_line == high, term, 0.0)
    left = jnp.concatenate([part.astype(F32) for part in three_parts(term)], axis=0).astype(BF)
    sums = lax.dot_general(left, lanes, NT, preferred_element_type=F32)
    sums = sums[0:8] + sums[8:16] + sums[16:24]
    rows = [jnp.concatenate([sums[k : k + 1] for k in range(at, at + 4)], axis=1) for at in (0, 4)]
    return rows


def edge_kernel(
    anomalies, base, observed, obs_scale, obs_rows, edge,
    base_edge, observed_all, scale_all, rows_all, sems,
):
    border = pl.ds(S - EDGE, EDGE)
    copies = [
        pltpu.make_async_copy(obs_rows, rows_all, sems.at[0]),
        pltpu.make_async_copy(obs_scale, scale_all, sems.at[1]),
        pltpu.make_async_copy(observed, observed_all, sems.at[2]),
        pltpu.make_async_copy(base.at[:, border], base_edge, sems.at[3]),
        pltpu.make_async_copy(anomalies.at[:, border], edge.at[pl.ds(0, ROWS)], sems.at[4]),
    ]
    for copy in copies:
        copy.start()
    for copy in copies[:4]:
        copy.wait()
    weight, value = sums_at_rows(
        S // 128 - 4, observed_all[...], scale_all[...], rows_all[...] - spot()[0] * S
    )
    empty = jnp.zeros((1, EDGE - REACH), F32)
    extra = list(three_parts(base_edge[...]))
    for row in (weight, value):
        extra += three_parts(jnp.concatenate([empty, row], axis=1))
    extra.append(jnp.zeros((7, EDGE), BF))
    edge[ROWS:] = jnp.concatenate(extra, axis=0)
    copies[4].wait()


def banded(rows, band, first, count):
    total = jnp.zeros((count * PITCH, CH), F32)
    for k in range(TILES):
        at = (first + k) * PITCH
        total = total + jnp.dot(
            rows[at : at + count * PITCH],
            band[k * CH : k * CH + CH],
            preferred_element_type=F32,
        )
    return total


def put_chunk(total, k, chunk, out, means):
    at = k * PITCH
    out[chunk // 2, :, chunk % 2 * CH : chunk % 2 * CH + CH] = total[at : at + ROWS].astype(BF)
    at = at + ROWS
    means[:, chunk * CH : chunk * CH + CH] = (
        total[at : at + 1] + total[at + 1 : at + 2] + total[at + 2 : at + 3]
    )


def inner_kernel(offsets, anomalies, base, transform, out, band, border, means, rows, sems):
    copies = [
        pltpu.make_async_copy(transform, out.at[k, :, pl.ds(COLS, M)], sems.at[k])
        for k in range(GROUP)
    ]
    for copy in copies:
        copy.start()
    for k in range(S // CH):
        c = slice(k * CH, k * CH + CH)
        at = k * PITCH
        rows[at : at + ROWS] = anomalies[:, c]
        rows[at + ROWS : at + PITCH] = base_rows(base[:, c])
    for k in range(TILES):
        shift = (
            lax.broadcasted_iota(jnp.int32, (CH, CH), 0)
            - lax.broadcasted_iota(jnp.int32, (CH, CH), 1)
            + (k * CH - REACH)
        )
        count = jnp.zeros((CH, CH), F32)
        for tap in range(TAPS):
            count = count + jnp.where(shift == offsets[tap], 1.0 / TAPS, 0.0)
        band[k * CH : k * CH + CH] = count.astype(BF)
    total = banded(rows, band, 0, INNER)
    means[...] = jnp.zeros_like(means)
    for k in range(INNER):
        put_chunk(total, k, k + OUTER, out, means)
    for k in range(OUTER):
        border[k * 16 : k * 16 + 16] = rows[k * PITCH + ROWS : (k + 1) * PITCH]
    for copy in copies:
        copy.wait()


def outer_kernel(
    edge, first, band, border, means_in, out_in, out, base_mean, rows, means, chunks, sems
):
    state, column, _, _ = spot()
    whole = state > 0
    means[...] = means_in[...]
    for k in range(OUTER):
        at = k * PITCH
        rows[at : at + PITCH] = edge[:, k * CH : k * CH + CH]
        at = at + OUTER * PITCH
        rows[at : at + ROWS] = first[:, k * CH : k * CH + CH]
        rows[at + ROWS : at + PITCH] = border[k * 16 : k * 16 + 16]
    seen = jnp.where(whole, 1.0, 0.0).astype(BF)
    before = rows[2 * PITCH : 4 * PITCH]
    after = rows[4 * PITCH : 6 * PITCH]
    rows[4 * PITCH : 6 * PITCH] = after * seen
    total = banded(rows, band, 0, 2)
    for k in range(2):
        put_chunk(total, k, k, chunks, means)
    rows[4 * PITCH : 6 * PITCH] = after
    rows[2 * PITCH : 4 * PITCH] = before * seen
    total = banded(rows, band, 2, 2)
    for k in range(2):
        put_chunk(total, k, k + 2, chunks, means)
    copies = [
        pltpu.make_async_copy(chunks.at[k], out.at[k, :, pl.ds(0, COLS)], sems.at[k])
        for k in range(2)
    ]
    for copy in copies:
        copy.start()
    for copy in copies:
        copy.wait()
    base_mean[...] = means[:, pl.ds(pl.multiple_of(column * COLS, COLS), COLS)]


def weight_kernel(observed, obs_scale, obs_rows, edge, weight_row, value_row):
    state, column, _, _ = spot()
    weight, value = sums_at_rows(
        (column - 1) * 4, observed[...], obs_scale[...], obs_rows[...] - state * S
    )
    half = pl.ds(EDGE - REACH, REACH)
    row = lambda k: edge[ROWS : ROWS + 16, half][k : k + 1].astype(F32)
    mine = column > 0
    for own, target, at in ((weight, weight_row, 3), (value, value_row, 6)):
        sent = row(at) + row(at + 1) + row(at + 2)
        target[...] = jnp.where(mine, own, sent)


def two_part_rows(value, count):
    high = value.astype(BF).astype(F32)
    low = value - high
    row = jnp.concatenate([high, low], axis=1)
    return jnp.concatenate([row, jnp.zeros((count - 1, 128), F32)], axis=0).astype(BF)


def seated_lanes(y_hi):
    lane = lax.broadcasted_iota(jnp.int32, (16, 128), 1)
    return (lane >= 16 + 32 * y_hi) & (lane < 24 + 32 * y_hi)


def seated(slopes):
    lane = lax.broadcasted_iota(jnp.int32, (16, 128), 1)
    mine = ((lane & (ROWS - 1)) >> 2) == lax.broadcasted_iota(jnp.int32, (16, 128), 0)
    high = slopes.astype(BF).astype(F32)
    low = slopes - high
    spread = []
    for j in range(GROUP):
        c = slice(j * ROWS, j * ROWS + ROWS)
        row = jnp.concatenate([high[:, c], low[:, c]], axis=1)
        spread.append(jnp.where(mine, row, 0.0))
    source = lax.broadcasted_iota(jnp.int32, (128, 128), 0)
    target = 16 + (source & 3) + jnp.where(source >= ROWS, 4, 0)
    pick = lax.broadcasted_iota(jnp.int32, (128, 128), 1) == target
    pick = jnp.where(pick, 1.0, 0.0).astype(BF)
    return jnp.dot(
        jnp.concatenate(spread, axis=0).astype(BF), pick, preferred_element_type=F32
    )


def first_half(tile, y_hi):
    return jnp.where(y_hi == 0, tile, pltpu.roll(tile, 96, 1))


def read_seats(tile, y_hi):
    tile = first_half(tile, y_hi)
    lane = lax.broadcasted_iota(jnp.int32, (16, ROWS), 1)
    row = lax.broadcasted_iota(jnp.int32, (16, ROWS), 0)
    sums = jnp.zeros((16, ROWS), F32)
    for q in range(4):
        part = tile[:, 16 + q : 17 + q] + tile[:, 20 + q : 21 + q]
        sums = sums + jnp.where((lane >> 2 == row) & (lane & 3 == q), part, 0.0)
    return jnp.sum(sums, axis=0, keepdims=True)


def refill_seats(tile, y_hi):
    tile = first_half(tile, y_hi)
    tall = jnp.concatenate([tile, jnp.zeros((112, 128), F32)], axis=0).T
    tile = jnp.where(seated_lanes(0), pltpu.roll(tall[64:80], 16, 1), tile)
    return jnp.where(y_hi == 0, tile, pltpu.roll(tile, 32, 1))


def gram_kernel(
    mine, other, base_mean, weight_row, value_row,
    out, gathered, scaled, part,
):
    core = lax.axis_index("core")
    crossed = jnp.where(spot()[1] * COLS < EDGE, GROUP // 2, 0)
    for k in range(GROUP):
        for block, side in ((mine, core), (other, 1 - core)):
            home = lax.rem(k + crossed, GROUP) * 128 + side * ROWS
            gathered[pl.ds(pl.multiple_of(home, ROWS), ROWS)] = block[k, :, 0:COLS]

    half = GROUP * ROWS
    for k in range(COLS // CH):
        c = slice(k * CH, k * CH + CH)
        predicted = []
        for block in (mine, other):
            mean = jnp.dot(
                block[:, :, COLS:].reshape(half, M), gathered[:, c], preferred_element_type=F32
            )
            mean = mean + base_mean[:, c]
            predicted.append(mean + 0.25 * mean * mean)
        average = jnp.sum(predicted[0] + predicted[1], axis=0, keepdims=True) * (1.0 / M)
        weight = weight_row[:, c]
        root = jnp.sqrt(weight * (1.0 / (M - 1)))
        slope = (value_row[:, c] - weight * average) * (1.0 / math.sqrt(M - 1))
        for n in range(2):
            difference = predicted[n] - average
            scaled[n * half : n * half + half, c] = (difference * root).astype(BF)
            if n == 0:
                product = difference * slope
                product = product[:, :128] + product[:, 128:]
                if k == 0:
                    part[...] = product
                else:
                    part[...] += product
    slopes = jnp.sum(part[...].T, axis=0, keepdims=True)
    left_half = lax.broadcasted_iota(jnp.int32, (16, 128), 1) < ROWS
    seats = seated(slopes)
    gram = lax.dot_general(scaled[...], scaled[0:half], NT, preferred_element_type=F32)
    here = [core == n for n in range(2)]
    for j in range(GROUP):
        lanes = slice(j // 2 * 128, j // 2 * 128 + 128)
        seat = seats[j * 16 : j * 16 + 16]
        for y_hi in range(2):
            target = out.at[y_hi * GROUP + j]
            for z in range(16):
                at = z // 2 * ROWS + y_hi * 32
                both = jnp.where(
                    here[z % 2], gram[at : at + 32, lanes], gram[half + at : half + at + 32, lanes]
                )
                top, bottom = both[0:16], both[16:32]
                if j % 2 == 0:
                    packed = jnp.where(left_half, top, pltpu.roll(bottom, ROWS, 1))
                else:
                    packed = jnp.where(left_half, pltpu.roll(top, ROWS, 1), bottom)
                if z // 2 == j:
                    taken = seated_lanes(y_hi) & (core == z % 2)
                    packed = jnp.where(taken, pltpu.roll(seat, 32, 1) if y_hi else seat, packed)
                target[z * 16 : z * 16 + 16] = packed.astype(BF)


def middle_kernel(parts, out, total):
    for first in range(0, 256, 64):
        rows = slice(first, first + 64)
        sums = parts[0, rows].astype(F32)
        for k in range(1, 2 * GROUP):
            sums = sums + parts[k, rows].astype(F32)
        total[rows] = sums
        for z in range(first // 16, first // 16 + 4):
            at = z * 16 - first
            out[z, 0:16] = sums[at : at + 16].astype(BF)
    block = spot()[2] // ROWS
    at = pl.ds(pl.multiple_of(block * 16, 16), 16)
    tail = two_part_rows(read_seats(total[at], lax.axis_index("y_hi")), 16)
    for z in range(16):
        out[z, 16:32] = tail


def last_kernel(parts, weights, hessian, gradient, packed):
    _, _, row0, column0 = spot()
    total = parts[0].astype(F32)
    for z in range(1, 16):
        total = total + parts[z].astype(F32)
    packed[...] = total[0:16]

    @pl.when(lax.axis_index("z") == row0 // ROWS)
    def _():
        packed[...] = refill_seats(packed[...], lax.axis_index("y_hi"))

    row = lax.broadcasted_iota(jnp.int32, (16, ROWS), 1) + row0
    column = lax.broadcasted_iota(jnp.int32, (16, ROWS), 0) + column0
    for half in range(2):
        block = packed[:, half * ROWS : half * ROWS + ROWS]
        same = row == column + half * 16
        hessian[half * 16 : half * 16 + 16] = block + jnp.where(same, 1.0, 0.0)
    gradient[...] = weights[...] - (total[16:17, 0:ROWS] + total[16:17, ROWS:])


def on_device(base_state, anomalies, transform, weights, observed, obs_scale, obs_rows, offsets):
    row = lambda v: v.reshape(1, S)
    base = row(base_state)
    obs = (row(observed), row(obs_scale), row(obs_rows))

    edge = call(
        edge_kernel,
        shape(PITCH, EDGE),
        [hbm()] * 5,
        scratch=[
            pltpu.VMEM((1, EDGE), F32),
            pltpu.VMEM((1, S), F32),
            pltpu.VMEM((1, S), F32),
            pltpu.VMEM((1, S), jnp.int32),
            pltpu.SemaphoreType.DMA((5,)),
        ],
        flops=4 * 10**9,
        nbytes=MIB,
        limit=FULL,
    )(anomalies, base, *obs)
    onward = [(d, (d + 2) % 64 ^ 1) for d in range(64)]
    edge = lax.ppermute(edge, ("z", "y_hi", "y_lo"), onward)
    first = lax.ppermute(anomalies[:, :EDGE], "y_lo", [(0, 1), (1, 0)])

    outgoing, band, border, means = call(
        inner_kernel,
        (
            shape(GROUP, ROWS, COLS + M),
            shape(TILES * CH, CH),
            shape(OUTER * 16, CH),
            shape32(1, S),
        ),
        [smem()] + [vmem()] * 2 + [hbm()],
        scratch=[
            pltpu.VMEM((S // CH * PITCH, CH), BF),
            pltpu.SemaphoreType.DMA((GROUP,)),
        ],
        flops=2 * INNER * PITCH * TILES * CH * CH,
        nbytes=4 * MIB,
    )(offsets, anomalies, base, transform)
    anywhere = pl.BlockSpec(memory_space=pl.ANY)
    outgoing, base_mean = call(
        outer_kernel,
        (shape(GROUP, ROWS, COLS + M), shape32(1, COLS)),
        [vmem()] * 5 + [anywhere],
        scratch=[
            pltpu.VMEM((2 * OUTER * PITCH, CH), BF),
            pltpu.VMEM((1, S), F32),
            pltpu.VMEM((2, ROWS, COLS), BF),
            pltpu.SemaphoreType.DMA((2,)),
        ],
        flops=2 * OUTER * PITCH * TILES * CH * CH,
        nbytes=MIB,
        alias={5: 0},
        out_specs=(anywhere, vmem()),
    )(edge, first, band, border, means, outgoing)

    mine = lax.all_to_all(outgoing, ("y_lo", "x"), 0, 0)
    other = lax.ppermute(mine, "core", [(0, 1), (1, 0)])

    weight_row, value_row = call(
        weight_kernel,
        (shape32(1, COLS), shape32(1, COLS)),
        [vmem()] * 4,
        flops=2 * 48 * S * 128,
        nbytes=MIB,
    )(*obs, edge)

    parts = call(
        gram_kernel,
        shape(2 * GROUP, 256, 128),
        [vmem()] * 5,
        scratch=[
            pltpu.VMEM((M, COLS), BF),
            pltpu.VMEM((M, COLS), BF),
            pltpu.VMEM((GROUP * ROWS, 128), F32),
        ],
        flops=2 * M * M * 768,
        nbytes=4 * MIB,
        limit=32,
    )(mine, other, base_mean, weight_row, value_row)
    parts = lax.all_to_all(parts, ("y_hi", "y_lo", "x"), 0, 0)
    sums = call(
        middle_kernel,
        shape(16, 32, 128),
        [vmem()],
        scratch=[pltpu.VMEM((256, 128), F32)],
        nbytes=MIB,
    )(parts)
    sums = lax.all_to_all(sums, "z", 0, 0)
    hessian, gradient = call(
        last_kernel, (shape32(32, ROWS), shape32(1, ROWS)), [vmem()] * 2, nbytes=MIB // 4,
        scratch=[pltpu.VMEM((16, 128), F32)],
    )(sums, weights.reshape(1, ROWS))
    return hessian.T, gradient.reshape(ROWS)


def solution(mesh):
    fine = Mesh(mesh.devices.reshape(16, 2, 2, 4, 2), ("z", "y_hi", "y_lo", "x", "core"))
    state = ("z", "y_hi")
    member = ("y_lo", "x", "core")
    placed = (
        P(state),
        P(member, state),
        P(member, None),
        P(member),
        P(state),
        P(state),
        P(state),
        P(),
    )
    return jax.shard_map(
        on_device,
        mesh=fine,
        in_specs=placed,
        out_specs=(P(member, state), P(member)),
        check_vma=False,
    )
```
